32 devices in a mesh: groups: 2 (over y), roll: 4 (over z), tp: 2 (over x), seq: 2 (over core).
Axes of the slice: x: 2, y: 2, z: 4, core: 2. Of those that a mesh axis runs over, the one named last changes fastest.
Arguments:
- hidden: bfloat16 [128, 8192], P('groups', ('roll', 'seq')), parts along dimension 0, may hold values from -6 to 6
- w_query: bfloat16 [8192, 8192], P(('roll', 'seq'), 'tp'), may hold values from -0.0625 to 0.0625
- w_key: bfloat16 [8192, 1024], P(('roll', 'seq'), 'tp'), may hold values from -0.0625 to 0.0625
- w_value: bfloat16 [8192, 1024], P(('roll', 'seq'), 'tp'), may hold values from -0.0625 to 0.0625
- b_query: bfloat16 [8192], P('tp'), may hold values from -12 to 12
- b_key: bfloat16 [1024], P('tp'), may hold values from -12 to 12
- b_value: bfloat16 [1024], P('tp'), may hold values from -6 to 6
- w_out: bfloat16 [8192, 8192], P('tp', ('roll', 'seq')), may hold values from -0.0625 to 0.0625
- prefix_keys: bfloat16 [4, 4096, 1024], P('groups', ('roll', 'seq'), 'tp'), parts along dimension 0, may hold values from -256 to 256
- prefix_values: bfloat16 [4, 4096, 1024], P('groups', ('roll', 'seq'), 'tp'), parts along dimension 0, may hold values from -6 to 6
- suffix_keys: bfloat16 [16, 2048, 1024], P(('groups', 'roll'), 'seq', 'tp'), parts along dimension 0, may hold values from -6 to 6
- suffix_values: bfloat16 [16, 2048, 1024], P(('groups', 'roll'), 'seq', 'tp'), parts along dimension 0, may hold values from -6 to 6
- suffix_lengths: int32 [16], P('groups'), parts along dimension 0, may hold values from 1 to 2048, 8192 in all
- prompt_of: int32 [16], P('groups'), parts along dimension 0, may hold values from 0 to 1, as said below
Outputs:
- attended: bfloat16 [128, 8192], P(('groups', 'tp'), ('roll', 'seq')), parts along dimension 0
The draws below stay inside these ranges and needn't reach their ends.
There are 2 independent parts, one for each index of `groups`. The reference program is written for one: setup_inputs(seed, part) draws one part's arguments, and reference() takes and returns one part's arrays. A program takes and returns all parts, laid end to end along the dimension named above; an argument that names none is the same for every part. Nothing has to cross between parts.
Inputs may be any that keep to these rules, and one draw needn't show every extreme that they name: Only the first suffix_lengths[r] rows of a rollout's suffix cache are live; the lengths of a group add up to 8192 and the largest is exactly 2048. `prompt_of`: every prompt is extended by exactly 4 rollouts.
All inputs are finite; a program needn't handle non-finite values.
Results may differ from the reference program's by a relative error of at most 0.009.
The reference program's roundings to bfloat16 on the way (of `query`, `key_new`, `value_new` and `attention`) count: a program that leaves them out, or rounds other values in their place, can miss the bound.
Values may be sent and summed in bfloat16 or wider, within the bound.
A program may use at most 128 MiB of HBM per device.

```python
import math
import jax
import jax.numpy as jnp
import numpy as np
from jax import lax

D = 8192
H = 64
KVH = 8
HD = 128
PROMPTS = 2
GUESS = 8
PREFIX = 4096
ROLLOUTS = 8
SUFFIX = 2048
TOKENS = 64


def draw_prefix_keys(key, part):
    base = jnp.clip(jax.random.normal(key, (PROMPTS, PREFIX, KVH * HD), jnp.float32), -8.0, 8.0)
    return base.astype(jnp.bfloat16)


def draw_prompt_of(key, part):
    return (jax.random.permutation(key, ROLLOUTS) % PROMPTS).astype(jnp.int32)


def block_scale(rng, dims, shards, least, top_value):
    loudness, own = 1.0, jax.random.fold_in(rng, 6)
    for axis_at, shards_of in shards:
        steps = jnp.exp(jax.random.uniform(jax.random.fold_in(own, axis_at), (shards_of,), jnp.float32, least / len(shards), top_value / len(shards)))
        loudness = loudness * jnp.repeat(steps, dims[axis_at] // shards_of).reshape([-1 if axis == axis_at else 1 for axis in range(len(dims))])
    return loudness


def profile(number_of, total, bound, lean):
    loads = [(1 << 20) // math.isqrt(rank ** lean) + 1 for rank in range(2, number_of + 1)]
    spare, counts = total - bound - (number_of - 1), [1] * (number_of - 1)
    while spare > 0:
        movable = [i for i in range(number_of - 1) if counts[i] < bound]
        pool, budget = sum([loads[i] for i in movable]), spare
        for i in movable:
            extra = min(bound - counts[i], max(1, budget * loads[i] // pool), spare)
            counts[i] = counts[i] + extra
            spare = spare - extra
    return np.array([bound] + counts)


def uneven_parts(key, number_of, total, bound, slope):
    if number_of == 2:
        one = jax.random.randint(key, (), max(1, total - bound), min(bound, total - 1) + 1)
        return jnp.stack([one, total - one])
    lengths = jnp.asarray(profile(number_of, total, bound, slope), jnp.int32)
    pairs = (number_of - 1) // 2
    giver, receiver = lengths[1:1 + 2 * pairs:2], lengths[2:2 + 2 * pairs:2]
    slack = jnp.minimum(giver - 1, bound - receiver)
    passed = jax.random.randint(jax.random.fold_in(key, 1), (pairs,), 0, 1 << 20) % (slack + 1)
    lengths = lengths.at[1:1 + 2 * pairs:2].set(giver - passed).at[2:2 + 2 * pairs:2].set(receiver + passed)
    return lengths[jax.random.permutation(jax.random.fold_in(key, 2), number_of)]


def scatter_about(rng, shape, deviation, bound, pieces=(), held_as=jnp.bfloat16):
    values = jax.random.normal(rng, shape, jnp.float32) * deviation
    if len(pieces) > 0:
        values = block_scale(rng, shape, pieces, -0.22, 0.18) * values
    return jnp.clip(values, min=-bound, max=bound).astype(held_as)


def setup_inputs(seed: int = 0, part: int = 0) -> dict:
    arg_keys = jax.random.split(jax.random.key(seed), 15)
    own_keys = jax.random.split(jax.random.fold_in(arg_keys[14], part), 15)
    hidden = scatter_about(own_keys[0], (TOKENS, D), 1.0, 6.0, ((1, 8),))
    w_query = scatter_about(arg_keys[1], (D, H * HD), D ** -0.5, 0.0625, ((0, 8), (1, 2)))
    w_key = scatter_about(arg_keys[2], (D, KVH * HD), D ** -0.5, 0.0625, ((0, 8), (1, 2)))
    w_value = scatter_about(arg_keys[3], (D, KVH * HD), D ** -0.5, 0.0625, ((0, 8), (1, 2)))
    b_query = scatter_about(arg_keys[4], (H * HD,), 3.0, 12.0, ((0, 2),))
    b_key = scatter_about(arg_keys[5], (KVH * HD,), 3.0, 12.0, ((0, 2),))
    b_value = scatter_about(arg_keys[6], (KVH * HD,), 1.0, 6.0, ((0, 2),))
    w_out = scatter_about(arg_keys[7], (H * HD, D), (H * HD) ** -0.5, 0.0625, ((0, 2), (1, 8)))
    prefix_keys = draw_prefix_keys(jax.random.fold_in(jax.random.fold_in(arg_keys[14], part), 71), part)
    prefix_values = scatter_about(own_keys[9], (PROMPTS, PREFIX, KVH * HD), 1.0, 6.0, ((1, 8), (2, 2)))
    suffix_keys = scatter_about(own_keys[10], (ROLLOUTS, SUFFIX, KVH * HD), 1.0, 6.0, ((0, 4), (1, 2), (2, 2)))
    suffix_values = scatter_about(own_keys[11], (ROLLOUTS, SUFFIX, KVH * HD), 1.0, 6.0, ((0, 4), (1, 2), (2, 2)))
    suffix_lengths = uneven_parts(own_keys[12], ROLLOUTS, ROLLOUTS * SUFFIX // 2, SUFFIX, 2).astype(jnp.int32)
    prompt_of = draw_prompt_of(jax.random.fold_in(jax.random.fold_in(arg_keys[14], part), 71), part)
    return dict(hidden=hidden, w_query=w_query, w_key=w_key, w_value=w_value, b_query=b_query, b_key=b_key, b_value=b_value, w_out=w_out, prefix_keys=prefix_keys, prefix_values=prefix_values, suffix_keys=suffix_keys, suffix_values=suffix_values, suffix_lengths=suffix_lengths, prompt_of=prompt_of)


ROPE_BASE = 1000000.0

def rotate(values, positions):
    half = values.shape[-1] // 2
    steps = jnp.arange(half).astype(jnp.float32) * (2.0 / values.shape[-1])
    freqs = jnp.exp(-math.log(ROPE_BASE) * steps)
    angles = positions[:, None] * freqs[None, :]
    cosine = jnp.cos(angles)[:, None, :]
    sine = jnp.sin(angles)[:, None, :]
    first = values[..., :half]
    second = values[..., half:]
    return jnp.concatenate([first * cosine - second * sine, second * cosine + first * sine], axis=-1)

def project(hidden, weight, bias):
    return jnp.dot(hidden, weight, preferred_element_type=jnp.float32) + bias.astype(jnp.float32)

def reference(hidden, w_query, w_key, w_value, b_query, b_key, b_value, w_out, prefix_keys, prefix_values, suffix_keys, suffix_values, suffix_lengths, prompt_of):
    row_count = hidden.shape[0]
    group = H // KVH
    row_ids = jnp.arange(row_count, dtype=jnp.int32)
    owners = row_ids // GUESS
    offsets = row_ids % GUESS
    positions = (PREFIX + suffix_lengths[owners] + offsets).astype(jnp.float32)
    query = rotate(project(hidden, w_query, b_query).reshape(row_count, H, HD), positions).astype(jnp.bfloat16)
    key_new = rotate(project(hidden, w_key, b_key).reshape(row_count, KVH, HD), positions).astype(jnp.bfloat16)
    value_new = project(hidden, w_value, b_value).astype(jnp.bfloat16).reshape(row_count, KVH, HD)
    scale = 1.0 / math.sqrt(HD)
    key_ids = jnp.arange(PREFIX + SUFFIX + GUESS, dtype=jnp.int32)
    guess_ids = jnp.arange(GUESS, dtype=jnp.int32)

    def one_rollout(rollout):
        start = (rollout * GUESS).astype(jnp.int32)
        prompt = prompt_of[rollout].astype(jnp.int32)
        queries = lax.dynamic_slice_in_dim(query, start, GUESS, 0).astype(jnp.float32).reshape(GUESS, KVH, group, HD)
        keys = jnp.concatenate([lax.dynamic_index_in_dim(prefix_keys, prompt, 0, keepdims=False).astype(jnp.float32).reshape(PREFIX, KVH, HD), lax.dynamic_index_in_dim(suffix_keys, rollout, 0, keepdims=False).astype(jnp.float32).reshape(SUFFIX, KVH, HD), lax.dynamic_slice_in_dim(key_new, start, GUESS, 0).astype(jnp.float32)], axis=0)
        values = jnp.concatenate([lax.dynamic_index_in_dim(prefix_values, prompt, 0, keepdims=False).astype(jnp.float32).reshape(PREFIX, KVH, HD), lax.dynamic_index_in_dim(suffix_values, rollout, 0, keepdims=False).astype(jnp.float32).reshape(SUFFIX, KVH, HD), lax.dynamic_slice_in_dim(value_new, start, GUESS, 0).astype(jnp.float32)], axis=0)
        length = suffix_lengths[rollout]
        in_suffix = key_ids - PREFIX < length
        in_guess = key_ids[None, :] - (PREFIX + SUFFIX) <= guess_ids[:, None]
        visible = jnp.where((key_ids < PREFIX)[None, :], True, jnp.where((key_ids < PREFIX + SUFFIX)[None, :], in_suffix[None, :], in_guess))
        scores = jnp.einsum('tkgd,skd->tkgs', queries, keys) * scale
        scores = jnp.where(visible[:, None, None, :], scores, -jnp.inf)
        peak = lax.optimization_barrier(jnp.max(scores, axis=-1))
        weights = jnp.exp(scores - peak[..., None])
        total = lax.optimization_barrier(jnp.sum(weights, axis=-1))
        rounded = lax.optimization_barrier(weights.astype(jnp.bfloat16)).astype(jnp.float32)
        output = jnp.einsum('tkgs,skd->tkgd', rounded, values) / total[..., None]
        return output.reshape(GUESS, H * HD)
    attention = lax.map(one_rollout, jnp.arange(ROLLOUTS, dtype=jnp.int32))
    attention = attention.reshape(row_count, H * HD).astype(jnp.bfloat16)
    return jnp.dot(attention, w_out, preferred_element_type=jnp.float32).astype(jnp.bfloat16)
```

```python
import functools
import math

import jax
import jax.numpy as jnp
import numpy as np
from jax import lax
from jax.experimental import pallas as pl
from jax.experimental.pallas import tpu as pltpu
from jax.sharding import PartitionSpec as P

HD = 128
GUESS = 8
ROPE_BASE = 1000000.0
NEG_FILL = -1e30
SCALE = 1.0 / math.sqrt(HD)
MESH = pl.DeviceIdType.MESH
F32 = jnp.float32
BF16 = jnp.bfloat16


def dot(a, b):
    return jnp.dot(a, b, preferred_element_type=F32)


def dot_nt(a, b):
    return lax.dot_general(a, b, (((1,), (1,)), ((), ())), preferred_element_type=F32)


def kernel(
    dims,
    lens_ref,
    prompt_ref,
    freq_ref,
    bq_ref,
    bk_ref,
    bv_ref,
    hid_ref,
    wq_ref,
    wk_ref,
    wv_ref,
    wo_ref,
    pk_ref,
    pv_ref,
    sk_ref,
    sv_ref,
    out_ref,
    hid,
    wq,
    wk,
    wv,
    wo,
    kb,
    vb,
    skb,
    svb,
    vt,
    svt,
    sibout,
    sibin,
    zs,
    zin,
    qg,
    kn,
    vn,
    onum,
    ostat,
    nsend,
    nin,
    stsend,
    stin,
    att,
    acc,
    tin,
    ld,
    ldw,
    ldo,
    sw_s,
    sw_r,
    pr_s,
    pr_r,
    rs_s,
    rs_r,
    ag_s,
    ag_r,
    nu_s,
    nu_r,
    st_s,
    st_r,
    at_s,
    at_r,
    fw_s,
    fw_r,
    tp_s,
    tp_r,
):
    R, T = dims["R"], dims["T"]
    kvw, gq, rz, M = dims["kvw"], dims["gq"], dims["rz"], dims["M"]
    kvh, qhalf, pre, suf = dims["kvh"], dims["qhalf"], dims["pre"], dims["suf"]
    prompts, per = dims["prompts"], dims["per"]
    gw = gq * HD
    cw = gw + 2 * HD
    W = kvw * HD
    L = gq * rz
    mt = M // T
    z = lax.axis_index("roll")
    c = lax.axis_index("seq")
    t = lax.axis_index("tp")
    sib = 1 - c

    def kv_off(core):
        if kvh >= 2:
            return pl.multiple_of(core * W, HD)
        return 0

    def q_off(core, k):
        return pl.multiple_of((core * qhalf + k * gq) * HD, HD)

    halves = (sib, c)

    loads = [pltpu.make_async_copy(hid_ref, hid, ld.at[0])]
    loads[0].start()
    wload = {}
    for s in range(2):
        a = pltpu.make_async_copy(wk_ref.at[:, pl.ds(kv_off(halves[s]), W)], wk.at[s], ld.at[1 + s])
        b = pltpu.make_async_copy(wv_ref.at[:, pl.ds(kv_off(halves[s]), W)], wv.at[s], ld.at[3 + s])
        for k in range(kvw):
            wload[s, k] = pltpu.make_async_copy(
                wq_ref.at[:, pl.ds(q_off(halves[s], k), gw)], wq.at[s, k], ldw.at[s, k]
            )
            wload[s, k].start()
            if k == 0:
                a.start()
                b.start()
        loads += [a, b]

    barrier = pltpu.get_barrier_semaphore()
    for o in range(1, R):
        pl.semaphore_signal(
            barrier, inc=1, device_id={"roll": lax.rem(z + o, R)}, device_id_type=MESH
        )
    pl.semaphore_signal(barrier, inc=1, device_id={"seq": sib}, device_id_type=MESH)
    for o in range(1, T):
        pl.semaphore_signal(
            barrier, inc=1, device_id={"tp": lax.rem(t + o, T)}, device_id_type=MESH
        )
    pl.semaphore_wait(barrier, R + T - 1)

    def project(s, k):
        x = hid[...]
        cols = slice(k * HD, (k + 1) * HD)
        return dot(x, wq[s, k]), dot(x, wk[s, :, cols]), dot(x, wv[s, :, cols])

    pairs = []
    loads[0].wait()
    for k in range(kvw):
        wload[0, k].wait()
        if k == 0:
            loads[1].wait()
            loads[2].wait()
        a, b, d = project(0, k)
        sibout[k, :, 0:gw] = a
        sibout[k, :, gw : gw + HD] = b
        sibout[k, :, gw + HD : cw] = d
        cp = pltpu.make_async_remote_copy(
            sibout.at[k], sibin.at[k], pr_s.at[k], pr_r.at[k],
            device_id={"seq": sib}, device_id_type=MESH,
        )
        cp.start()
        pairs.append(cp)

    kv_local, kv_remote = [], []
    for i, (src, dst) in enumerate(((pk_ref, kb), (pv_ref, vb), (sk_ref, skb), (sv_ref, svb))):
        cp = pltpu.make_async_copy(
            src.at[:, :, pl.ds(kv_off(c), W)], dst.at[0], ld.at[5 + i]
        )
        cp.start()
        kv_local.append(cp)
        cp = pltpu.make_async_remote_copy(
            src.at[:, :, pl.ds(kv_off(sib), W)], dst.at[1], sw_s.at[i], sw_r.at[i],
            device_id={"seq": sib}, device_id_type=MESH,
        )
        cp.start()
        kv_remote.append(cp)
    oload = {}
    for s, half in ((0, c), (1, sib)):
        for k in range(kvw):
            oload[s, k] = pltpu.make_async_copy(
                wo_ref.at[pl.ds(q_off(half, k), gw)], wo.at[s, k], ldo.at[s, k]
            )
            oload[s, k].start()

    def along(src_of, dst_of, sems, semr, o):
        dest = lax.rem(z + o, R)
        return pltpu.make_async_remote_copy(
            src_of(dest), dst_of(z), sems, semr, device_id={"roll": dest}, device_id_type=MESH
        )

    def arrived(dst_of, sems, semr, o):
        source = lax.rem(z + R - o, R)
        ref = dst_of(source)
        pltpu.make_async_remote_copy(
            ref, ref, sems, semr, device_id={"roll": lax.rem(z + o, R)}, device_id_type=MESH
        ).wait_recv()
        return source

    sends = []

    for k in range(kvw):
        wload[1, k].wait()
        if k == 0:
            loads[3].wait()
            loads[4].wait()
        a, b, d = project(1, k)
        pairs[k].wait()
        zs[k, :, 0:gw] = a + sibin[k, :, 0:gw]
        zs[k, :, gw : gw + HD] = b + sibin[k, :, gw : gw + HD]
        zs[k, :, gw + HD : cw] = d + sibin[k, :, gw + HD : cw]
        for o in range(1, R):
            cp = along(
                lambda dest, k=k: zs.at[k, pl.ds(pl.multiple_of(dest * rz, rz), rz)],
                lambda me, k=k: zin.at[k, me],
                rs_s.at[k, o], rs_r.at[k, o], o,
            )
            cp.start()
            sends.append(cp)

    tok = lax.broadcasted_iota(jnp.int32, (rz, HD), 0)
    base = jnp.zeros((rz, HD), jnp.int32)
    for i in range(per):
        base = jnp.where(tok // GUESS == i, lens_ref[z * per + i], base)
    position = (dims["prefix_total"] + base + tok % GUESS).astype(F32)
    angles = position * freq_ref[...]
    cosine = jnp.cos(angles)
    lane = lax.broadcasted_iota(jnp.int32, (rz, HD), 1)
    sine = jnp.sin(angles)
    sine = jnp.where(lane < HD // 2, -sine, sine)

    def rotate(x):
        return x * cosine + pltpu.roll(x, HD // 2, 1) * sine

    for cp in kv_local:
        cp.wait()
    for cp in kv_remote:
        cp.wait()
    for k in range(kvw):
        cols = slice(k * HD, (k + 1) * HD)
        for s in range(2):
            for p in range(prompts):
                vt[k, p * HD : (p + 1) * HD, s * pre : (s + 1) * pre] = vb[s, p, :, cols].T
            for p in range(per):
                svt[k, p * HD : (p + 1) * HD, s * suf : (s + 1) * suf] = svb[s, p, :, cols].T

    for k in range(kvw):
        for o in range(1, R):
            arrived(lambda src, k=k: zin.at[k, src], rs_s.at[k, o], rs_r.at[k, o], o)
        x = zs[k, pl.ds(pl.multiple_of(z * rz, rz), rz), :]
        for o in range(1, R):
            x = x + zin[k, lax.rem(z + R - o, R)]
        xq = x[:, :gw] + bq_ref[:, pl.ds(q_off(c, k), gw)].astype(F32)
        kcol = pl.ds(pl.multiple_of(kv_off(c) + k * HD, HD), HD)
        for h in range(gq):
            qg[k, z, h] = rotate(xq[:, h * HD : (h + 1) * HD]).astype(BF16)
        for o in range(1, R):
            cp = along(
                lambda dest, k=k: qg.at[k, z], lambda me, k=k: qg.at[k, me],
                ag_s.at[k, o], ag_r.at[k, o], o,
            )
            cp.start()
            sends.append(cp)
        kn[k] = rotate(x[:, gw : gw + HD] + bk_ref[:, kcol].astype(F32))
        vn[k] = x[:, gw + HD :] + bv_ref[:, kcol].astype(F32)

    toks = lax.broadcasted_iota(jnp.int32, (rz, HD), 0)
    parts = [(toks // GUESS == i).astype(F32).astype(BF16) for i in range(per)]
    ltok = lax.broadcasted_iota(jnp.int32, (1, L), 1) % rz
    live = jnp.zeros((1, L), jnp.int32)
    for i in range(per):
        live = jnp.where(ltok // GUESS == i, lens_ref[z * per + i], live)
    for k in range(kvw):
        cols = slice(k * HD, (k + 1) * HD)
        q = qg[k, z]
        keys = jnp.concatenate(
            [jnp.concatenate([skb[s, p, :, cols] for p in range(per)], axis=1) for s in range(2)],
            axis=0,
        )
        qs = jnp.concatenate([(q * m[None]).reshape(L, HD) for m in parts], axis=1)
        s_suf = dot_nt(keys, qs)
        place = lax.broadcasted_iota(jnp.int32, (2 * suf, L), 0)
        place = (place + c * suf) % (2 * suf)
        s_suf = jnp.where(place < live, s_suf, NEG_FILL)
        s_new = dot_nt(kn[k].astype(BF16), q.reshape(L, HD))
        row = lax.broadcasted_iota(jnp.int32, (rz, L), 0)
        col = lax.broadcasted_iota(jnp.int32, (rz, L), 1) % rz
        seen = (row // GUESS == col // GUESS) & (row % GUESS <= col % GUESS)
        s_new = jnp.where(seen, s_new, NEG_FILL)
        peak = jnp.maximum(
            jnp.max(s_suf, axis=0, keepdims=True), jnp.max(s_new, axis=0, keepdims=True)
        )
        w_suf = jnp.exp((s_suf - peak) * SCALE)
        w_new = jnp.exp((s_new - peak) * SCALE)
        both = dot(svt[k], w_suf.astype(BF16))
        numer = dot(vn[k].T.astype(BF16), w_new.astype(BF16))
        for i in range(per):
            numer = numer + jnp.where(ltok // GUESS == i, both[i * HD : (i + 1) * HD], 0.0)
        onum[k] = numer
        ostat[k, 0:1, :] = peak
        ostat[k, 1:2, :] = jnp.sum(w_suf, axis=0, keepdims=True) + jnp.sum(
            w_new, axis=0, keepdims=True
        )

    zb = max(1, min(R, 256 // L))
    for k in range(kvw):
        cols = slice(k * HD, (k + 1) * HD)
        for o in range(1, R):
            arrived(lambda src, k=k: qg.at[k, src], ag_s.at[k, o], ag_r.at[k, o], o)
        keys = jnp.concatenate(
            [
                jnp.concatenate([kb[s, p, :, cols] for p in range(prompts)], axis=1)
                for s in range(2)
            ],
            axis=0,
        )
        for first in range(0, R, zb):
            blocks = []
            pick = jnp.zeros((1, zb * L), jnp.int32)
            wide = lax.broadcasted_iota(jnp.int32, (1, zb * L), 1)
            for j in range(zb):
                owner = jnp.zeros((rz, HD), jnp.int32)
                for i in range(per):
                    which = prompt_ref[(first + j) * per + i]
                    owner = jnp.where(toks // GUESS == i, which, owner)
                    here = (wide // L == j) & ((wide % rz) // GUESS == i)
                    pick = jnp.where(here, which, pick)
                q = qg[k, first + j]
                blocks.append(
                    jnp.concatenate(
                        [
                            (q * (owner == p).astype(F32).astype(BF16)[None]).reshape(L, HD)
                            for p in range(prompts)
                        ],
                        axis=1,
                    )
                )
            s_pre = dot_nt(keys, jnp.concatenate(blocks, axis=0))
            peak = jnp.max(s_pre, axis=0, keepdims=True)
            w_pre = jnp.exp((s_pre - peak) * SCALE)
            total = jnp.sum(w_pre, axis=0, keepdims=True)
            both = dot(vt[k], w_pre.astype(BF16))
            numer = jnp.zeros((HD, zb * L), F32)
            for p in range(prompts):
                numer = jnp.where(pick == p, both[p * HD : (p + 1) * HD], numer)
            numer = numer.astype(BF16)
            for j in range(zb):
                nsend[k, first + j] = numer[:, j * L : (j + 1) * L]
                stsend[k, first + j, 0:1, :] = peak[:, j * L : (j + 1) * L]
                stsend[k, first + j, 1:2, :] = total[:, j * L : (j + 1) * L]
        for o in range(1, R):
            cp = along(
                lambda dest, k=k: nsend.at[k, dest], lambda me, k=k: nin.at[k, me],
                nu_s.at[k, o], nu_r.at[k, o], o,
            )
            cp.start()
            sends.append(cp)
            cp = along(
                lambda dest, k=k: stsend.at[k, dest], lambda me, k=k: stin.at[k, me],
                st_s.at[k, o], st_r.at[k, o], o,
            )
            cp.start()
            sends.append(cp)

    forwards = []

    def forward(k, o, place):
        rows = pl.ds(pl.multiple_of(place * rz, rz), rz)
        cp = pltpu.make_async_remote_copy(
            att.at[0, k, rows], att.at[1, k, rows], fw_s.at[k, o], fw_r.at[k, o],
            device_id={"seq": sib}, device_id_type=MESH,
        )
        cp.start()
        forwards.append(cp)

    for k in range(kvw):
        for o in range(1, R):
            arrived(lambda src, k=k: nin.at[k, src], nu_s.at[k, o], nu_r.at[k, o], o)
            arrived(lambda src, k=k: stin.at[k, src], st_s.at[k, o], st_r.at[k, o], o)
        stats = [(ostat[k, 0:1, :], ostat[k, 1:2, :]), (stsend[k, z, 0:1, :], stsend[k, z, 1:2, :])]
        numers = [onum[k], nsend[k, z].astype(F32)]
        for o in range(1, R):
            source = lax.rem(z + R - o, R)
            stats.append((stin[k, source, 0:1, :], stin[k, source, 1:2, :]))
            numers.append(nin[k, source].astype(F32))
        top = functools.reduce(jnp.maximum, [peak for peak, _ in stats])
        total = jnp.zeros((1, L), F32)
        numer = jnp.zeros((HD, L), F32)
        for (peak, part), piece in zip(stats, numers):
            factor = jnp.exp((peak - top) * SCALE)
            total = total + part * factor
            numer = numer + piece * factor
        share = (numer / total).T.astype(BF16)
        mine = pl.ds(pl.multiple_of(z * rz, rz), rz)
        att[0, k, mine, :] = jnp.concatenate(
            [share[h * rz : (h + 1) * rz] for h in range(gq)], axis=1
        )
        for o in range(1, R):
            cp = along(
                lambda dest, k=k: att.at[0, k, mine],
                lambda me, k=k: att.at[0, k, pl.ds(pl.multiple_of(me * rz, rz), rz)],
                at_s.at[k, o], at_r.at[k, o], o,
            )
            cp.start()
            sends.append(cp)
        forward(k, 0, z)

    total = jnp.zeros(acc.shape, F32)
    for k in range(kvw):
        for o in range(1, R):
            source = arrived(
                lambda src, k=k: att.at[0, k, pl.ds(pl.multiple_of(src * rz, rz), rz)],
                at_s.at[k, o], at_r.at[k, o], o,
            )
            forward(k, o, source)
        oload[0, k].wait()
        total = total + dot(att[0, k], wo[0, k])
    for cp in forwards:
        cp.wait()
    for k in range(kvw):
        oload[1, k].wait()
        total = total + dot(att[1, k], wo[1, k])
    acc[...] = total

    tps = []
    for o in range(1, T):
        dest = lax.rem(t + o, T)
        cp = pltpu.make_async_remote_copy(
            acc.at[pl.ds(pl.multiple_of(dest * mt, mt), mt)], tin.at[o - 1],
            tp_s.at[o], tp_r.at[o], device_id={"tp": dest}, device_id_type=MESH,
        )
        cp.start()
        tps.append(cp)
    result = acc[pl.ds(pl.multiple_of(t * mt, mt), mt), :]
    for o in range(1, T):
        tps[o - 1].wait()
        result = result + tin[o - 1]
    out_ref[...] = result.astype(BF16)
    for cp in sends:
        cp.wait_send()


def body(
    sizes,
    hidden,
    w_query,
    w_key,
    w_value,
    b_query,
    b_key,
    b_value,
    w_out,
    prefix_keys,
    prefix_values,
    suffix_keys,
    suffix_values,
    suffix_lengths,
    prompt_of,
):
    R, S, T = sizes
    M, K = hidden.shape
    q_heads, kvh = w_query.shape[1] // HD, w_key.shape[1] // HD
    prompts, pre, _ = prefix_keys.shape
    per, suf, _ = suffix_keys.shape
    N = w_out.shape[1]
    qhalf = q_heads // S
    kvw = max(kvh // S, 1)
    gq = qhalf // kvw
    rz = per * GUESS
    dims = dict(
        R=R, T=T, M=M, kvw=kvw, gq=gq, rz=rz, kvh=kvh, qhalf=qhalf, pre=pre, suf=suf,
        prompts=prompts, per=per, prefix_total=pre * R * S,
    )
    W, gw, L = kvw * HD, gq * HD, gq * rz
    cw = gw + 2 * HD
    steps = np.arange(HD // 2).astype(np.float32) * np.float32(2.0 / HD)
    freqs = np.exp(np.float32(-math.log(ROPE_BASE)) * steps).astype(np.float32)
    freqs = jnp.asarray(np.concatenate([freqs, freqs])[None])
    smem = pl.BlockSpec(memory_space=pltpu.SMEM)
    vmem = pl.BlockSpec(memory_space=pltpu.VMEM)
    hbm = pl.BlockSpec(memory_space=pl.ANY)
    dma = pltpu.SemaphoreType.DMA
    return pl.pallas_call(
        functools.partial(kernel, dims),
        out_shape=jax.ShapeDtypeStruct((M // T, N), BF16),
        in_specs=[smem, smem] + [vmem] * 4 + [hbm] * 9,
        out_specs=vmem,
        scratch_shapes=[
            pltpu.VMEM((M, K), BF16),
            pltpu.VMEM((S, kvw, K, gw), BF16),
            pltpu.VMEM((S, K, W), BF16),
            pltpu.VMEM((S, K, W), BF16),
            pltpu.VMEM((S, kvw, gw, N), BF16),
            pltpu.VMEM((S, prompts, pre, W), BF16),
            pltpu.VMEM((S, prompts, pre, W), BF16),
            pltpu.VMEM((S, per, suf, W), BF16),
            pltpu.VMEM((S, per, suf, W), BF16),
            pltpu.VMEM((kvw, prompts * HD, S * pre), BF16),
            pltpu.VMEM((kvw, per * HD, S * suf), BF16),
            pltpu.VMEM((kvw, M, cw), F32),
            pltpu.VMEM((kvw, M, cw), F32),
            pltpu.VMEM((kvw, M, cw), F32),
            pltpu.VMEM((kvw, R, rz, cw), F32),
            pltpu.VMEM((kvw, R, gq, rz, HD), BF16),
            pltpu.VMEM((kvw, rz, HD), F32),
            pltpu.VMEM((kvw, rz, HD), F32),
            pltpu.VMEM((kvw, HD, L), F32),
            pltpu.VMEM((kvw, 8, L), F32),
            pltpu.VMEM((kvw, R, HD, L), BF16),
            pltpu.VMEM((kvw, R, HD, L), BF16),
            pltpu.VMEM((kvw, R, 8, L), F32),
            pltpu.VMEM((kvw, R, 8, L), F32),
            pltpu.VMEM((S, kvw, M, gw), BF16),
            pltpu.VMEM((M, N), F32),
            pltpu.VMEM((max(T - 1, 1), M // T, N), F32),
            dma((9,)),
            dma((S, kvw)),
            dma((S, kvw)),
            dma((4,)),
            dma((4,)),
            dma((kvw,)),
            dma((kvw,)),
        ]
        + [dma((kvw, R))] * 12
        + [dma((T,))] * 2,
        compiler_params=pltpu.CompilerParams(
            collective_id=0, has_side_effects=True, vmem_limit_bytes=60 * 1024 * 1024
        ),
        cost_estimate=pl.CostEstimate(
            flops=2 * M * K * (w_query.shape[1] + 2 * w_key.shape[1]) + 2 * M * N * w_out.shape[0],
            bytes_accessed=2 * (w_query.size + 2 * w_key.size + w_out.size)
            + 4 * (prefix_keys.size + suffix_keys.size),
            transcendentals=0,
        ),
    )(
        suffix_lengths,
        prompt_of,
        freqs,
        b_query[None],
        b_key[None],
        b_value[None],
        hidden,
        w_query,
        w_key,
        w_value,
        w_out,
        prefix_keys,
        prefix_values,
        suffix_keys,
        suffix_values,
    )


def solution(mesh):
    sizes = (mesh.shape["roll"], mesh.shape["seq"], mesh.shape["tp"])
    return jax.shard_map(
        functools.partial(body, sizes),
        mesh=mesh,
        in_specs=(
            P("groups", ("roll", "seq")),
            P(("roll", "seq"), "tp"),
            P(("roll", "seq"), "tp"),
            P(("roll", "seq"), "tp"),
            P("tp"),
            P("tp"),
            P("tp"),
            P("tp", ("roll", "seq")),
            P("groups", ("roll", "seq"), "tp"),
            P("groups", ("roll", "seq"), "tp"),
            P(("groups", "roll"), "seq", "tp"),
            P(("groups", "roll"), "seq", "tp"),
            P("groups"),
            P("groups"),
        ),
        out_specs=P(("groups", "tp"), ("roll", "seq")),
        check_vma=False,
    )
```

```python
import functools
import math

import jax
import jax.numpy as jnp
import numpy as np
from jax import lax
from jax.experimental import pallas as pl
from jax.experimental.pallas import tpu as pltpu
from jax.sharding import PartitionSpec as P

HD = 128
GUESS = 8
ROPE_BASE = 1000000.0
NEG_FILL = -1e30
SCALE = 1.0 / math.sqrt(HD)
MESH = pl.DeviceIdType.MESH
F32 = jnp.float32
BF16 = jnp.bfloat16


def dot(a, b):
    return jnp.dot(a, b, preferred_element_type=F32)


def dot_nt(a, b):
    return lax.dot_general(a, b, (((1,), (1,)), ((), ())), preferred_element_type=F32)


def kernel(
    dims,
    lens_ref,
    prompt_ref,
    freq_ref,
    bq_ref,
    bk_ref,
    bv_ref,
    hid_ref,
    wq_ref,
    wk_ref,
    wv_ref,
    wo_ref,
    pk_ref,
    pv_ref,
    sk_ref,
    sv_ref,
    out_ref,
    hid,
    wq,
    wk,
    wv,
    wo,
    kb,
    vb,
    skb,
    svb,
    vt,
    svt,
    sibout,
    sibin,
    zs,
    zq,
    zin,
    qg,
    kn,
    vn,
    onum,
    ostat,
    nsend,
    nin,
    stsend,
    stin,
    att,
    acc,
    tin,
    bq,
    bk,
    bv,
    ld,
    ldw,
    ldo,
    sw_s,
    sw_r,
    pr_s,
    pr_r,
    rs_s,
    rs_r,
    ag_s,
    ag_r,
    nu_s,
    nu_r,
    st_s,
    st_r,
    at_s,
    at_r,
    fw_s,
    fw_r,
    tp_s,
    tp_r,
):
    R, T = dims["R"], dims["T"]
    kvw, gq, rz, M = dims["kvw"], dims["gq"], dims["rz"], dims["M"]
    kvh, qhalf, pre, suf = dims["kvh"], dims["qhalf"], dims["pre"], dims["suf"]
    prompts, per = dims["prompts"], dims["per"]
    gw = gq * HD
    cw = gw + 2 * HD
    W = kvw * HD
    L = gq * rz
    mt = M // T
    z = lax.axis_index("roll")
    c = lax.axis_index("seq")
    t = lax.axis_index("tp")
    sib = 1 - c

    def kv_off(core):
        if kvh >= 2:
            return pl.multiple_of(core * W, HD)
        return 0

    def q_off(core, k):
        return pl.multiple_of((core * qhalf + k * gq) * HD, HD)

    halves = (sib, c)
    hk = gq + 2
    biases = ((bq_ref, bq), (bk_ref, bk), (bv_ref, bv))

    loads = [pltpu.make_async_copy(hid_ref, hid, ld.at[0])]
    loads[0].start()
    wload = {}
    for k in range(kvw):
        for s in range(2):
            cols = pl.ds(q_off(halves[s], k), gw)
            wload[s, k] = pltpu.make_async_copy(wq_ref.at[:, cols], wq.at[s, k], ldw.at[s, k])
            wload[s, k].start()
            if k == 0:
                cols = pl.ds(kv_off(halves[s]), W)
                for src, dst, i in ((wk_ref, wk, 1), (wv_ref, wv, 3)):
                    cp = pltpu.make_async_copy(src.at[:, cols], dst.at[s], ld.at[i + s])
                    cp.start()
                    loads.append(cp)

    barrier = pltpu.get_barrier_semaphore()
    for o in range(1, R):
        pl.semaphore_signal(
            barrier, inc=1, device_id={"roll": lax.rem(z + o, R)}, device_id_type=MESH
        )
    pl.semaphore_signal(barrier, inc=1, device_id={"seq": sib}, device_id_type=MESH)
    for o in range(1, T):
        pl.semaphore_signal(
            barrier, inc=1, device_id={"tp": lax.rem(t + o, T)}, device_id_type=MESH
        )
    pl.semaphore_wait(barrier, R + T - 1)

    def project(s, k):
        x = hid[...]
        cols = slice(k * HD, (k + 1) * HD)
        return dot(x, wq[s, k]), dot(x, wk[s, :, cols]), dot(x, wv[s, :, cols])

    def other_half(k):
        wload[0, k].wait()
        if k == 0:
            loads[1].wait()
            loads[2].wait()
        a, b, d = project(0, k)
        sibout[k, :, 0:gw] = a
        sibout[k, :, gw : gw + HD] = b
        sibout[k, :, gw + HD : cw] = d
        cp = pltpu.make_async_remote_copy(
            sibout.at[k], sibin.at[k], pr_s.at[k], pr_r.at[k],
            device_id={"seq": sib}, device_id_type=MESH,
        )
        cp.start()
        return cp

    def own_half(k):
        wload[1, k].wait()
        if k == 0:
            loads[3].wait()
            loads[4].wait()
        a, b, d = project(1, k)
        zs[k, :, 0:gw] = a
        zs[k, :, gw : gw + HD] = b
        zs[k, :, gw + HD : cw] = d

    loads[0].wait()
    pairs = [other_half(0)]
    own_half(0)
    for k in range(1, kvw):
        pairs.append(other_half(k))

    kv_local, kv_remote = [], []
    for i, (src, dst) in enumerate(((pk_ref, kb), (pv_ref, vb), (sk_ref, skb), (sv_ref, svb))):
        cp = pltpu.make_async_copy(
            src.at[:, :, pl.ds(kv_off(c), W)], dst.at[0], ld.at[5 + i]
        )
        cp.start()
        kv_local.append(cp)
        cp = pltpu.make_async_remote_copy(
            src.at[:, :, pl.ds(kv_off(sib), W)], dst.at[1], sw_s.at[i], sw_r.at[i],
            device_id={"seq": sib}, device_id_type=MESH,
        )
        cp.start()
        kv_remote.append(cp)
    oload = {}
    for s, half in ((0, c), (1, sib)):
        for k in range(kvw):
            oload[s, k] = pltpu.make_async_copy(
                wo_ref.at[pl.ds(q_off(half, k), gw)], wo.at[s, k], ldo.at[s, k]
            )
            oload[s, k].start()

    def along(src_of, dst_of, sems, semr, o):
        dest = lax.rem(z + o, R)
        return pltpu.make_async_remote_copy(
            src_of(dest), dst_of(z), sems, semr, device_id={"roll": dest}, device_id_type=MESH
        )

    def arrived(dst_of, sems, semr, o):
        source = lax.rem(z + R - o, R)
        ref = dst_of(source)
        pltpu.make_async_remote_copy(
            ref, ref, sems, semr, device_id={"roll": lax.rem(z + o, R)}, device_id_type=MESH
        ).wait_recv()
        return source

    sends = []

    wlane = lax.broadcasted_iota(jnp.int32, (M, HD), 1)
    for k in range(kvw):
        if k > 0:
            own_half(k)
        pairs[k].wait()
        powers = jnp.zeros((M, HD), F32)
        for h in range(hk):
            cols = slice(h * HD, (h + 1) * HD)
            x = zs[k, :, cols] + sibin[k, :, cols]
            zs[k, :, cols] = x
            largest = jnp.maximum(jnp.max(jnp.abs(x), axis=1, keepdims=True), 1e-30)
            power = jnp.ceil(jnp.log2(largest) + 0.01)
            code = jnp.round(x * (32767.0 / jnp.exp2(power)))
            zq[k, :, cols] = code.astype(jnp.int32).astype(jnp.int16)
            powers = jnp.where(wlane == h, power, powers)
        zq[k, :, cw : cw + HD] = powers.astype(jnp.int32).astype(jnp.int16)
        for o in range(1, R):
            cp = along(
                lambda dest, k=k: zq.at[k, pl.ds(pl.multiple_of(dest * rz, rz), rz)],
                lambda me, k=k: zin.at[k, me],
                rs_s.at[k, o], rs_r.at[k, o], o,
            )
            cp.start()
            sends.append(cp)
    for src, dst in biases:
        dst[...] = src[...].astype(F32).reshape(dst.shape)

    tok = lax.broadcasted_iota(jnp.int32, (rz, HD), 0)
    base = jnp.zeros((rz, HD), jnp.int32)
    for i in range(per):
        base = jnp.where(tok // GUESS == i, lens_ref[z * per + i], base)
    position = (dims["prefix_total"] + base + tok % GUESS).astype(F32)
    angles = position * freq_ref[...]
    cosine = jnp.cos(angles)
    lane = lax.broadcasted_iota(jnp.int32, (rz, HD), 1)
    sine = jnp.sin(angles)
    sine = jnp.where(lane < HD // 2, -sine, sine)

    def rotate(x):
        return x * cosine + pltpu.roll(x, HD // 2, 1) * sine

    def turn(s):
        for k in range(kvw):
            cols = slice(k * HD, (k + 1) * HD)
            for p in range(prompts):
                vt[k, p * HD : (p + 1) * HD, s * pre : (s + 1) * pre] = vb[s, p, :, cols].T
            for p in range(per):
                svt[k, p * HD : (p + 1) * HD, s * suf : (s + 1) * suf] = svb[s, p, :, cols].T

    for cp in kv_local:
        cp.wait()
    turn(0)

    for k in range(kvw):
        for o in range(1, R):
            arrived(lambda src, k=k: zin.at[k, src], rs_s.at[k, o], rs_r.at[k, o], o)
        x = zs[k, pl.ds(pl.multiple_of(z * rz, rz), rz), :]
        sums = [x[:, h * HD : (h + 1) * HD] for h in range(hk)]
        for o in range(1, R):
            got = zin[k, lax.rem(z + R - o, R)].astype(jnp.int32).astype(F32)
            units = jnp.exp2(got[:, cw:]) * (1.0 / 32767.0)
            for h in range(hk):
                sums[h] = sums[h] + got[:, h * HD : (h + 1) * HD] * units[:, h : h + 1]
        x = jnp.concatenate(sums, axis=1)
        xq = x[:, :gw] + bq[:, pl.ds(q_off(c, k), gw)]
        kcol = pl.ds(pl.multiple_of(kv_off(c) + k * HD, HD), HD)
        for h in range(gq):
            qg[k, z, h] = rotate(xq[:, h * HD : (h + 1) * HD]).astype(BF16)
        for o in range(1, R):
            cp = along(
                lambda dest, k=k: qg.at[k, z], lambda me, k=k: qg.at[k, me],
                ag_s.at[k, o], ag_r.at[k, o], o,
            )
            cp.start()
            sends.append(cp)
        kn[k] = rotate(x[:, gw : gw + HD] + bk[:, kcol])
        vn[k] = x[:, gw + HD :] + bv[:, kcol]

    for cp in kv_remote:
        cp.wait()
    turn(1)

    toks = lax.broadcasted_iota(jnp.int32, (rz, HD), 0)
    parts = [(toks // GUESS == i).astype(F32).astype(BF16) for i in range(per)]
    ltok = lax.broadcasted_iota(jnp.int32, (1, L), 1) % rz
    live = jnp.zeros((1, L), jnp.int32)
    for i in range(per):
        live = jnp.where(ltok // GUESS == i, lens_ref[z * per + i], live)
    for k in range(kvw):
        cols = slice(k * HD, (k + 1) * HD)
        q = qg[k, z]
        keys = jnp.concatenate(
            [jnp.concatenate([skb[s, p, :, cols] for p in range(per)], axis=1) for s in range(2)],
            axis=0,
        )
        qs = jnp.concatenate([(q * m[None]).reshape(L, HD) for m in parts], axis=1)
        s_suf = dot_nt(keys, qs)
        place = lax.broadcasted_iota(jnp.int32, (2 * suf, L), 0)
        place = (place + c * suf) % (2 * suf)
        s_suf = jnp.where(place < live, s_suf, NEG_FILL)
        s_new = dot_nt(kn[k].astype(BF16), q.reshape(L, HD))
        row = lax.broadcasted_iota(jnp.int32, (rz, L), 0)
        col = lax.broadcasted_iota(jnp.int32, (rz, L), 1) % rz
        seen = (row // GUESS == col // GUESS) & (row % GUESS <= col % GUESS)
        s_new = jnp.where(seen, s_new, NEG_FILL)
        peak = jnp.maximum(
            jnp.max(s_suf, axis=0, keepdims=True), jnp.max(s_new, axis=0, keepdims=True)
        )
        w_suf = jnp.exp((s_suf - peak) * SCALE)
        w_new = jnp.exp((s_new - peak) * SCALE)
        both = dot(svt[k], w_suf.astype(BF16))
        numer = dot(vn[k].T.astype(BF16), w_new.astype(BF16))
        for i in range(per):
            numer = numer + jnp.where(ltok // GUESS == i, both[i * HD : (i + 1) * HD], 0.0)
        onum[k] = numer
        ostat[k, 0:1, :] = peak
        ostat[k, 1:2, :] = jnp.sum(w_suf, axis=0, keepdims=True) + jnp.sum(
            w_new, axis=0, keepdims=True
        )

    zb = max(1, min(R, 256 // L))
    for k in range(kvw):
        cols = slice(k * HD, (k + 1) * HD)
        keys = jnp.concatenate(
            [
                jnp.concatenate([kb[s, p, :, cols] for p in range(prompts)], axis=1)
                for s in range(2)
            ],
            axis=0,
        )
        for first in range(0, R, zb):
            blocks = []
            places = []
            for o in range(first, first + zb):
                if o == 0:
                    places.append(z)
                else:
                    places.append(
                        arrived(lambda src, k=k: qg.at[k, src], ag_s.at[k, o], ag_r.at[k, o], o)
                    )
            pick = jnp.zeros((1, zb * L), jnp.int32)
            wide = lax.broadcasted_iota(jnp.int32, (1, zb * L), 1)
            for j in range(zb):
                owner = jnp.zeros((rz, HD), jnp.int32)
                for i in range(per):
                    which = prompt_ref[places[j] * per + i]
                    owner = jnp.where(toks // GUESS == i, which, owner)
                    here = (wide // L == j) & ((wide % rz) // GUESS == i)
                    pick = jnp.where(here, which, pick)
                q = qg[k, places[j]]
                blocks.append(
                    jnp.concatenate(
                        [
                            (q * (owner == p).astype(F32).astype(BF16)[None]).reshape(L, HD)
                            for p in range(prompts)
                        ],
                        axis=1,
                    )
                )
            s_pre = dot_nt(keys, jnp.concatenate(blocks, axis=0))
            peak = jnp.max(s_pre, axis=0, keepdims=True)
            w_pre = jnp.exp((s_pre - peak) * SCALE)
            total = jnp.sum(w_pre, axis=0, keepdims=True)
            both = dot(vt[k], w_pre.astype(BF16))
            numer = jnp.zeros((HD, zb * L), F32)
            for p in range(prompts):
                numer = jnp.where(pick == p, both[p * HD : (p + 1) * HD], numer)
            numer = numer.astype(BF16)
            for j in range(zb):
                nsend[k, places[j]] = numer[:, j * L : (j + 1) * L]
                stsend[k, places[j], 0:1, :] = peak[:, j * L : (j + 1) * L]
                stsend[k, places[j], 1:2, :] = total[:, j * L : (j + 1) * L]
                o = R - first - j
                if o == R:
                    continue
                cp = along(
                    lambda dest, k=k: nsend.at[k, dest], lambda me, k=k: nin.at[k, me],
                    nu_s.at[k, o], nu_r.at[k, o], o,
                )
                cp.start()
                sends.append(cp)
                cp = along(
                    lambda dest, k=k: stsend.at[k, dest], lambda me, k=k: stin.at[k, me],
                    st_s.at[k, o], st_r.at[k, o], o,
                )
                cp.start()
                sends.append(cp)

    forwards = []

    def forward(k, o, place):
        rows = pl.ds(pl.multiple_of(place * rz, rz), rz)
        cp = pltpu.make_async_remote_copy(
            att.at[0, k, rows], att.at[1, k, rows], fw_s.at[k, o], fw_r.at[k, o],
            device_id={"seq": sib}, device_id_type=MESH,
        )
        cp.start()
        forwards.append(cp)

    for k in range(kvw):
        for o in range(1, R):
            arrived(lambda src, k=k: nin.at[k, src], nu_s.at[k, o], nu_r.at[k, o], o)
            arrived(lambda src, k=k: stin.at[k, src], st_s.at[k, o], st_r.at[k, o], o)
        stats = [(ostat[k, 0:1, :], ostat[k, 1:2, :]), (stsend[k, z, 0:1, :], stsend[k, z, 1:2, :])]
        numers = [onum[k], nsend[k, z].astype(F32)]
        for o in range(1, R):
            source = lax.rem(z + R - o, R)
            stats.append((stin[k, source, 0:1, :], stin[k, source, 1:2, :]))
            numers.append(nin[k, source].astype(F32))
        top = functools.reduce(jnp.maximum, [peak for peak, _ in stats])
        total = jnp.zeros((1, L), F32)
        numer = jnp.zeros((HD, L), F32)
        for (peak, part), piece in zip(stats, numers):
            factor = jnp.exp((peak - top) * SCALE)
            total = total + part * factor
            numer = numer + piece * factor
        share = (numer / total).T.astype(BF16)
        mine = pl.ds(pl.multiple_of(z * rz, rz), rz)
        att[0, k, mine, :] = jnp.concatenate(
            [share[h * rz : (h + 1) * rz] for h in range(gq)], axis=1
        )
        for o in range(1, R):
            cp = along(
                lambda dest, k=k: att.at[0, k, mine],
                lambda me, k=k: att.at[0, k, pl.ds(pl.multiple_of(me * rz, rz), rz)],
                at_s.at[k, o], at_r.at[k, o], o,
            )
            cp.start()
            sends.append(cp)
        forward(k, 0, z)

    total = jnp.zeros((M, dims["nb"] * acc.shape[2]), F32)
    for k in range(kvw):
        for o in range(1, R):
            source = arrived(
                lambda src, k=k: att.at[0, k, pl.ds(pl.multiple_of(src * rz, rz), rz)],
                at_s.at[k, o], at_r.at[k, o], o,
            )
            forward(k, o, source)
        oload[0, k].wait()
        total = total + dot(att[0, k], wo[0, k])
    for cp in forwards:
        cp.wait()
    for k in range(kvw):
        oload[1, k].wait()
    nb, nc = dims["nb"], acc.shape[2]
    tps = {}
    for n in range(nb):
        cols = slice(n * nc, (n + 1) * nc)
        piece = total[:, cols]
        for k in range(kvw):
            piece = piece + dot(att[1, k], wo[1, k, :, cols])
        acc[n] = piece
        for o in range(1, T):
            dest = lax.rem(t + o, T)
            tps[n, o] = pltpu.make_async_remote_copy(
                acc.at[n, pl.ds(pl.multiple_of(dest * mt, mt), mt)], tin.at[n, o - 1],
                tp_s.at[n, o], tp_r.at[n, o], device_id={"tp": dest}, device_id_type=MESH,
            )
            tps[n, o].start()
    for n in range(nb):
        result = acc[n, pl.ds(pl.multiple_of(t * mt, mt), mt), :]
        for o in range(1, T):
            tps[n, o].wait()
            result = result + tin[n, o - 1]
        out_ref[:, n * nc : (n + 1) * nc] = result.astype(BF16)
    for cp in sends:
        cp.wait_send()


def body(
    sizes,
    hidden,
    w_query,
    w_key,
    w_value,
    b_query,
    b_key,
    b_value,
    w_out,
    prefix_keys,
    prefix_values,
    suffix_keys,
    suffix_values,
    suffix_lengths,
    prompt_of,
):
    R, S, T = sizes
    M, K = hidden.shape
    q_heads, kvh = w_query.shape[1] // HD, w_key.shape[1] // HD
    prompts, pre, _ = prefix_keys.shape
    per, suf, _ = suffix_keys.shape
    N = w_out.shape[1]
    qhalf = q_heads // S
    kvw = max(kvh // S, 1)
    gq = qhalf // kvw
    rz = per * GUESS
    nb = 2 if N % (2 * HD) == 0 else 1
    dims = dict(
        R=R, T=T, M=M, kvw=kvw, gq=gq, rz=rz, kvh=kvh, qhalf=qhalf, pre=pre, suf=suf,
        prompts=prompts, per=per, prefix_total=pre * R * S, nb=nb,
    )
    W, gw, L = kvw * HD, gq * HD, gq * rz
    cw = gw + 2 * HD
    steps = np.arange(HD // 2).astype(np.float32) * np.float32(2.0 / HD)
    freqs = np.exp(np.float32(-math.log(ROPE_BASE)) * steps).astype(np.float32)
    freqs = jnp.asarray(np.concatenate([freqs, freqs])[None])
    smem = pl.BlockSpec(memory_space=pltpu.SMEM)
    vmem = pl.BlockSpec(memory_space=pltpu.VMEM)
    hbm = pl.BlockSpec(memory_space=pl.ANY)
    dma = pltpu.SemaphoreType.DMA
    return pl.pallas_call(
        functools.partial(kernel, dims),
        out_shape=jax.ShapeDtypeStruct((M // T, N), BF16),
        in_specs=[smem, smem] + [vmem] * 4 + [hbm] * 9,
        out_specs=vmem,
        scratch_shapes=[
            pltpu.VMEM((M, K), BF16),
            pltpu.VMEM((S, kvw, K, gw), BF16),
            pltpu.VMEM((S, K, W), BF16),
            pltpu.VMEM((S, K, W), BF16),
            pltpu.VMEM((S, kvw, gw, N), BF16),
            pltpu.VMEM((S, prompts, pre, W), BF16),
            pltpu.VMEM((S, prompts, pre, W), BF16),
            pltpu.VMEM((S, per, suf, W), BF16),
            pltpu.VMEM((S, per, suf, W), BF16),
            pltpu.VMEM((kvw, prompts * HD, S * pre), BF16),
            pltpu.VMEM((kvw, per * HD, S * suf), BF16),
            pltpu.VMEM((kvw, M, cw), F32),
            pltpu.VMEM((kvw, M, cw), F32),
            pltpu.VMEM((kvw, M, cw), F32),
            pltpu.VMEM((kvw, M, cw + HD), jnp.int16),
            pltpu.VMEM((kvw, R, rz, cw + HD), jnp.int16),
            pltpu.VMEM((kvw, R, gq, rz, HD), BF16),
            pltpu.VMEM((kvw, rz, HD), F32),
            pltpu.VMEM((kvw, rz, HD), F32),
            pltpu.VMEM((kvw, HD, L), F32),
            pltpu.VMEM((kvw, 8, L), F32),
            pltpu.VMEM((kvw, R, HD, L), BF16),
            pltpu.VMEM((kvw, R, HD, L), BF16),
            pltpu.VMEM((kvw, R, 8, L), F32),
            pltpu.VMEM((kvw, R, 8, L), F32),
            pltpu.VMEM((S, kvw, M, gw), BF16),
            pltpu.VMEM((nb, M, N // nb), F32),
            pltpu.VMEM((nb, max(T - 1, 1), M // T, N // nb), F32),
            pltpu.VMEM((1, q_heads * HD), F32),
            pltpu.VMEM((1, kvh * HD), F32),
            pltpu.VMEM((1, kvh * HD), F32),
            dma((9,)),
            dma((S, kvw)),
            dma((S, kvw)),
            dma((4,)),
            dma((4,)),
            dma((kvw,)),
            dma((kvw,)),
        ]
        + [dma((kvw, R))] * 12
        + [dma((nb, T))] * 2,
        compiler_params=pltpu.CompilerParams(
            collective_id=0, has_side_effects=True, vmem_limit_bytes=60 * 1024 * 1024
        ),
        cost_estimate=pl.CostEstimate(
            flops=2 * M * K * (w_query.shape[1] + 2 * w_key.shape[1]) + 2 * M * N * w_out.shape[0],
            bytes_accessed=2 * (w_query.size + 2 * w_key.size + w_out.size)
            + 4 * (prefix_keys.size + suffix_keys.size),
            transcendentals=0,
        ),
    )(
        suffix_lengths,
        prompt_of,
        freqs,
        b_query,
        b_key,
        b_value,
        hidden,
        w_query,
        w_key,
        w_value,
        w_out,
        prefix_keys,
        prefix_values,
        suffix_keys,
        suffix_values,
    )


def solution(mesh):
    sizes = (mesh.shape["roll"], mesh.shape["seq"], mesh.shape["tp"])
    return jax.shard_map(
        functools.partial(body, sizes),
        mesh=mesh,
        in_specs=(
            P("groups", ("roll", "seq")),
            P(("roll", "seq"), "tp"),
            P(("roll", "seq"), "tp"),
            P(("roll", "seq"), "tp"),
            P("tp"),
            P("tp"),
            P("tp"),
            P("tp", ("roll", "seq")),
            P("groups", ("roll", "seq"), "tp"),
            P("groups", ("roll", "seq"), "tp"),
            P(("groups", "roll"), "seq", "tp"),
            P(("groups", "roll"), "seq", "tp"),
            P("groups"),
            P("groups"),
        ),
        out_specs=P(("groups", "tp"), ("roll", "seq")),
        check_vma=False,
    )
```

```python
import functools
import math

import jax
import jax.numpy as jnp
import numpy as np
from jax import lax
from jax.experimental import pallas as pl
from jax.experimental.pallas import tpu as pltpu
from jax.sharding import PartitionSpec as P

HD = 128
GUESS = 8
ROPE_BASE = 1000000.0
NEG_FILL = -1e30
SCALE = math.log2(math.e) / math.sqrt(HD)
MESH = pl.DeviceIdType.MESH
F32 = jnp.float32
BF16 = jnp.bfloat16


def dot(a, b):
    return jnp.dot(a, b, preferred_element_type=F32)


def dot_nt(a, b):
    return lax.dot_general(a, b, (((1,), (1,)), ((), ())), preferred_element_type=F32)


def kernel(
    dims,
    lens_ref,
    prompt_ref,
    freq_ref,
    bq_ref,
    bk_ref,
    bv_ref,
    hid_ref,
    wq_ref,
    wk_ref,
    wv_ref,
    wo_ref,
    pk_ref,
    pv_ref,
    sk_ref,
    sv_ref,
    out_ref,
    hid,
    wq,
    wk,
    wv,
    wo,
    kb,
    vb,
    skb,
    svb,
    vt,
    svt,
    sibout,
    sibin,
    zs,
    zq,
    zin,
    qg,
    kn,
    vn,
    onum,
    ostat,
    nsend,
    nin,
    stsend,
    stin,
    att,
    acc,
    tin,
    bq,
    bk,
    bv,
    ld,
    ldw,
    ldo,
    sw_s,
    sw_r,
    pr_s,
    pr_r,
    rs_s,
    rs_r,
    ag_s,
    ag_r,
    nu_s,
    nu_r,
    st_s,
    st_r,
    at_s,
    at_r,
    fw_s,
    fw_r,
    tp_s,
    tp_r,
):
    R, T = dims["R"], dims["T"]
    kvw, gq, rz, M = dims["kvw"], dims["gq"], dims["rz"], dims["M"]
    kvh, qhalf, pre, suf = dims["kvh"], dims["qhalf"], dims["pre"], dims["suf"]
    prompts, per = dims["prompts"], dims["per"]
    gw = gq * HD
    cw = gw + 2 * HD
    W = kvw * HD
    L = gq * rz
    mt = M // T
    z = lax.axis_index("roll")
    c = lax.axis_index("seq")
    t = lax.axis_index("tp")
    sib = 1 - c

    def kv_off(core):
        if kvh >= 2:
            return pl.multiple_of(core * W, HD)
        return 0

    def q_off(core, k):
        return pl.multiple_of((core * qhalf + k * gq) * HD, HD)

    halves = (sib, c)
    hk = gq + 2
    biases = ((bq_ref, bq), (bk_ref, bk), (bv_ref, bv))

    loads = [pltpu.make_async_copy(hid_ref, hid, ld.at[0])]
    loads[0].start()
    wload = {}
    for k in range(kvw):
        for s in range(2):
            cols = pl.ds(q_off(halves[s], k), gw)
            wload[s, k] = pltpu.make_async_copy(wq_ref.at[:, cols], wq.at[s, k], ldw.at[s, k])
            wload[s, k].start()
            if k == 0:
                cols = pl.ds(kv_off(halves[s]), W)
                for src, dst, i in ((wk_ref, wk, 1), (wv_ref, wv, 3)):
                    cp = pltpu.make_async_copy(src.at[:, cols], dst.at[s], ld.at[i + s])
                    cp.start()
                    loads.append(cp)

    barrier = pltpu.get_barrier_semaphore()
    for o in range(1, R):
        pl.semaphore_signal(
            barrier, inc=1, device_id={"roll": lax.rem(z + o, R)}, device_id_type=MESH
        )
    pl.semaphore_signal(barrier, inc=1, device_id={"seq": sib}, device_id_type=MESH)
    for o in range(1, T):
        pl.semaphore_signal(
            barrier, inc=1, device_id={"tp": lax.rem(t + o, T)}, device_id_type=MESH
        )
    pl.semaphore_wait(barrier, R + T - 1)

    def project(s, k):
        x = hid[...]
        cols = slice(k * HD, (k + 1) * HD)
        return dot(x, wq[s, k]), dot(x, wk[s, :, cols]), dot(x, wv[s, :, cols])

    def other_half(k):
        wload[0, k].wait()
        if k == 0:
            loads[1].wait()
            loads[2].wait()
        a, b, d = project(0, k)
        sibout[k, :, 0:gw] = a
        sibout[k, :, gw : gw + HD] = b
        sibout[k, :, gw + HD : cw] = d
        cp = pltpu.make_async_remote_copy(
            sibout.at[k], sibin.at[k], pr_s.at[k], pr_r.at[k],
            device_id={"seq": sib}, device_id_type=MESH,
        )
        cp.start()
        return cp

    def own_half(k):
        wload[1, k].wait()
        if k == 0:
            loads[3].wait()
            loads[4].wait()
        a, b, d = project(1, k)
        zs[k, :, 0:gw] = a
        zs[k, :, gw : gw + HD] = b
        zs[k, :, gw + HD : cw] = d

    loads[0].wait()
    pairs = [other_half(0)]
    own_half(0)
    for k in range(1, kvw):
        pairs.append(other_half(k))

    kv_local, kv_remote = [], []
    for i, (src, dst) in enumerate(((pk_ref, kb), (pv_ref, vb), (sk_ref, skb), (sv_ref, svb))):
        cp = pltpu.make_async_copy(
            src.at[:, :, pl.ds(kv_off(c), W)], dst.at[0], ld.at[5 + i]
        )
        cp.start()
        kv_local.append(cp)
        cp = pltpu.make_async_remote_copy(
            src.at[:, :, pl.ds(kv_off(sib), W)], dst.at[1], sw_s.at[i], sw_r.at[i],
            device_id={"seq": sib}, device_id_type=MESH,
        )
        cp.start()
        kv_remote.append(cp)
    oload = {}
    for s, half in ((0, c), (1, sib)):
        for k in range(kvw):
            oload[s, k] = pltpu.make_async_copy(
                wo_ref.at[pl.ds(q_off(half, k), gw)], wo.at[s, k], ldo.at[s, k]
            )
            oload[s, k].start()

    def along(src_of, dst_of, sems, semr, o):
        dest = lax.rem(z + o, R)
        return pltpu.make_async_remote_copy(
            src_of(dest), dst_of(z), sems, semr, device_id={"roll": dest}, device_id_type=MESH
        )

    def arrived(dst_of, sems, semr, o):
        source = lax.rem(z + R - o, R)
        ref = dst_of(source)
        pltpu.make_async_remote_copy(
            ref, ref, sems, semr, device_id={"roll": lax.rem(z + o, R)}, device_id_type=MESH
        ).wait_recv()
        return source

    sends = []

    wlane = lax.broadcasted_iota(jnp.int32, (M, HD), 1)
    for k in range(kvw):
        if k > 0:
            own_half(k)
        pairs[k].wait()
        powers = jnp.zeros((M, HD), F32)
        for h in range(hk):
            cols = slice(h * HD, (h + 1) * HD)
            x = zs[k, :, cols] + sibin[k, :, cols]
            zs[k, :, cols] = x
            largest = jnp.maximum(jnp.max(jnp.abs(x), axis=1, keepdims=True), 1e-30)
            power = jnp.ceil(jnp.log2(largest) + 0.01)
            code = jnp.round(x * (32767.0 / jnp.exp2(power)))
            zq[k, :, cols] = code.astype(jnp.int32).astype(jnp.int16)
            powers = jnp.where(wlane == h, power, powers)
        zq[k, :, cw : cw + HD] = powers.astype(jnp.int32).astype(jnp.int16)
        for o in range(1, R):
            cp = along(
                lambda dest, k=k: zq.at[k, pl.ds(pl.multiple_of(dest * rz, rz), rz)],
                lambda me, k=k: zin.at[k, me],
                rs_s.at[k, o], rs_r.at[k, o], o,
            )
            cp.start()
            sends.append(cp)
    for src, dst in biases:
        dst[...] = src[...].astype(F32).reshape(dst.shape)

    tok = lax.broadcasted_iota(jnp.int32, (rz, HD), 0)
    base = jnp.zeros((rz, HD), jnp.int32)
    for i in range(per):
        base = jnp.where(tok // GUESS == i, lens_ref[z * per + i], base)
    position = (dims["prefix_total"] + base + tok % GUESS).astype(F32)
    angles = position * freq_ref[...]
    cosine = jnp.cos(angles)
    lane = lax.broadcasted_iota(jnp.int32, (rz, HD), 1)
    sine = jnp.sin(angles)
    sine = jnp.where(lane < HD // 2, -sine, sine)

    def rotate(x):
        return x * cosine + pltpu.roll(x, HD // 2, 1) * sine

    def turn(s):
        for k in range(kvw):
            cols = slice(k * HD, (k + 1) * HD)
            for p in range(prompts):
                vt[k, p * HD : (p + 1) * HD, s * pre : (s + 1) * pre] = vb[s, p, :, cols].T
            for p in range(per):
                svt[k, p * HD : (p + 1) * HD, s * suf : (s + 1) * suf] = svb[s, p, :, cols].T

    for cp in kv_local:
        cp.wait()
    turn(0)

    def finish(k):
        for o in range(1, R):
            arrived(lambda src, k=k: zin.at[k, src], rs_s.at[k, o], rs_r.at[k, o], o)
        x = zs[k, pl.ds(pl.multiple_of(z * rz, rz), rz), :]
        sums = [x[:, h * HD : (h + 1) * HD] for h in range(hk)]
        for o in range(1, R):
            got = zin[k, lax.rem(z + R - o, R)].astype(jnp.int32).astype(F32)
            units = jnp.exp2(got[:, cw:]) * (1.0 / 32767.0)
            for h in range(hk):
                sums[h] = sums[h] + got[:, h * HD : (h + 1) * HD] * units[:, h : h + 1]
        x = jnp.concatenate(sums, axis=1)
        xq = x[:, :gw] + bq[:, pl.ds(q_off(c, k), gw)]
        kcol = pl.ds(pl.multiple_of(kv_off(c) + k * HD, HD), HD)
        for h in range(gq):
            qg[k, z, h] = rotate(xq[:, h * HD : (h + 1) * HD]).astype(BF16)
        for o in range(1, R):
            cp = along(
                lambda dest, k=k: qg.at[k, z], lambda me, k=k: qg.at[k, me],
                ag_s.at[k, o], ag_r.at[k, o], o,
            )
            cp.start()
            sends.append(cp)
        kn[k] = rotate(x[:, gw : gw + HD] + bk[:, kcol])
        vn[k] = x[:, gw + HD :] + bv[:, kcol]

    toks = lax.broadcasted_iota(jnp.int32, (rz, HD), 0)
    parts = [(toks // GUESS == i).astype(F32).astype(BF16) for i in range(per)]
    ltok = lax.broadcasted_iota(jnp.int32, (1, L), 1) % rz
    live = jnp.zeros((1, L), jnp.int32)
    for i in range(per):
        live = jnp.where(ltok // GUESS == i, lens_ref[z * per + i], live)

    def own_rows(k):
        cols = slice(k * HD, (k + 1) * HD)
        q = qg[k, z]
        keys = jnp.concatenate(
            [jnp.concatenate([skb[s, p, :, cols] for p in range(per)], axis=1) for s in range(2)],
            axis=0,
        )
        qs = jnp.concatenate([(q * m[None]).reshape(L, HD) for m in parts], axis=1)
        s_suf = dot_nt(keys, qs)
        place = lax.broadcasted_iota(jnp.int32, (suf, L), 0)
        s_suf = jnp.concatenate(
            [
                jnp.where(place < live - half * suf, s_suf[s * suf : (s + 1) * suf], NEG_FILL)
                for s, half in ((0, c), (1, sib))
            ],
            axis=0,
        )
        s_new = dot_nt(kn[k].astype(BF16), q.reshape(L, HD))
        row = lax.broadcasted_iota(jnp.int32, (rz, L), 0)
        col = lax.broadcasted_iota(jnp.int32, (rz, L), 1) % rz
        seen = (row // GUESS == col // GUESS) & (row % GUESS <= col % GUESS)
        s_new = jnp.where(seen, s_new, NEG_FILL)
        peak = jnp.maximum(
            jnp.max(s_suf, axis=0, keepdims=True), jnp.max(s_new, axis=0, keepdims=True)
        )
        w_suf = jnp.exp2((s_suf - peak) * SCALE)
        w_new = jnp.exp2((s_new - peak) * SCALE)
        both = dot(svt[k], w_suf.astype(BF16))
        numer = dot(vn[k].T.astype(BF16), w_new.astype(BF16))
        for i in range(per):
            numer = numer + jnp.where(ltok // GUESS == i, both[i * HD : (i + 1) * HD], 0.0)
        onum[k] = numer
        ostat[k, 0:1, :] = peak
        ostat[k, 1:2, :] = jnp.sum(w_suf, axis=0, keepdims=True) + jnp.sum(
            w_new, axis=0, keepdims=True
        )

    zb = max(1, min(R, 256 // L))

    def every_row(k):
        cols = slice(k * HD, (k + 1) * HD)
        keys = jnp.concatenate(
            [
                jnp.concatenate([kb[s, p, :, cols] for p in range(prompts)], axis=1)
                for s in range(2)
            ],
            axis=0,
        )
        for first in range(0, R, zb):
            blocks = []
            places = []
            for o in range(first, first + zb):
                if o == 0:
                    places.append(z)
                else:
                    places.append(
                        arrived(lambda src, k=k: qg.at[k, src], ag_s.at[k, o], ag_r.at[k, o], o)
                    )
            pick = jnp.zeros((1, zb * L), jnp.int32)
            wide = lax.broadcasted_iota(jnp.int32, (1, zb * L), 1)
            for j in range(zb):
                owner = jnp.zeros((rz, HD), jnp.int32)
                for i in range(per):
                    which = prompt_ref[places[j] * per + i]
                    owner = jnp.where(toks // GUESS == i, which, owner)
                    here = (wide // L == j) & ((wide % rz) // GUESS == i)
                    pick = jnp.where(here, which, pick)
                q = qg[k, places[j]]
                blocks.append(
                    jnp.concatenate(
                        [
                            (q * (owner == p).astype(F32).astype(BF16)[None]).reshape(L, HD)
                            for p in range(prompts)
                        ],
                        axis=1,
                    )
                )
            s_pre = dot_nt(keys, jnp.concatenate(blocks, axis=0))
            peak = jnp.max(s_pre, axis=0, keepdims=True)
            w_pre = jnp.exp2((s_pre - peak) * SCALE)
            total = jnp.sum(w_pre, axis=0, keepdims=True)
            both = dot(vt[k], w_pre.astype(BF16))
            numer = jnp.zeros((HD, zb * L), F32)
            for p in range(prompts):
                numer = jnp.where(pick == p, both[p * HD : (p + 1) * HD], numer)
            numer = numer.astype(BF16)
            for j in range(zb):
                nsend[k, places[j]] = numer[:, j * L : (j + 1) * L]
                stsend[k, places[j], 0:1, :] = peak[:, j * L : (j + 1) * L]
                stsend[k, places[j], 1:2, :] = total[:, j * L : (j + 1) * L]
                o = R - first - j
                if o == R:
                    continue
                cp = along(
                    lambda dest, k=k: nsend.at[k, dest], lambda me, k=k: nin.at[k, me],
                    nu_s.at[k, o], nu_r.at[k, o], o,
                )
                cp.start()
                sends.append(cp)
                cp = along(
                    lambda dest, k=k: stsend.at[k, dest], lambda me, k=k: stin.at[k, me],
                    st_s.at[k, o], st_r.at[k, o], o,
                )
                cp.start()
                sends.append(cp)

    finish(0)
    for cp in kv_remote:
        cp.wait()
    turn(1)
    for k in range(1, kvw):
        finish(k)
    for k in range(kvw):
        every_row(k)
        own_rows(k)

    forwards = {}

    def forward(k, o, place):
        rows = pl.ds(pl.multiple_of(place * rz, rz), rz)
        cp = pltpu.make_async_remote_copy(
            att.at[0, k, rows], att.at[1, k, rows], fw_s.at[k, o], fw_r.at[k, o],
            device_id={"seq": sib}, device_id_type=MESH,
        )
        cp.start()
        forwards[k, o] = cp

    for k in range(kvw):
        for o in range(1, R):
            arrived(lambda src, k=k: nin.at[k, src], nu_s.at[k, o], nu_r.at[k, o], o)
            arrived(lambda src, k=k: stin.at[k, src], st_s.at[k, o], st_r.at[k, o], o)
        stats = [(ostat[k, 0:1, :], ostat[k, 1:2, :]), (stsend[k, z, 0:1, :], stsend[k, z, 1:2, :])]
        numers = [onum[k], nsend[k, z].astype(F32)]
        for o in range(1, R):
            source = lax.rem(z + R - o, R)
            stats.append((stin[k, source, 0:1, :], stin[k, source, 1:2, :]))
            numers.append(nin[k, source].astype(F32))
        top = functools.reduce(jnp.maximum, [peak for peak, _ in stats])
        total = jnp.zeros((1, L), F32)
        numer = jnp.zeros((HD, L), F32)
        for (peak, part), piece in zip(stats, numers):
            factor = jnp.exp2((peak - top) * SCALE)
            total = total + part * factor
            numer = numer + piece * factor
        share = (numer / total).T.astype(BF16)
        mine = pl.ds(pl.multiple_of(z * rz, rz), rz)
        att[0, k, mine, :] = jnp.concatenate(
            [share[h * rz : (h + 1) * rz] for h in range(gq)], axis=1
        )
        for o in range(1, R):
            cp = along(
                lambda dest, k=k: att.at[0, k, mine],
                lambda me, k=k: att.at[0, k, pl.ds(pl.multiple_of(me * rz, rz), rz)],
                at_s.at[k, o], at_r.at[k, o], o,
            )
            cp.start()
            sends.append(cp)
        forward(k, 0, z)

    total = jnp.zeros((M, dims["nb"] * acc.shape[2]), F32)
    for k in range(kvw):
        for o in range(1, R):
            source = arrived(
                lambda src, k=k: att.at[0, k, pl.ds(pl.multiple_of(src * rz, rz), rz)],
                at_s.at[k, o], at_r.at[k, o], o,
            )
            forward(k, o, source)
        oload[0, k].wait()
        total = total + dot(att[0, k], wo[0, k])
        for o in range(R):
            forwards[k, o].wait()
        oload[1, k].wait()
        if k < kvw - 1:
            total = total + dot(att[1, k], wo[1, k])
    nb, nc = dims["nb"], acc.shape[2]
    tps = {}
    for n in range(nb):
        cols = slice(n * nc, (n + 1) * nc)
        acc[n] = total[:, cols] + dot(att[1, kvw - 1], wo[1, kvw - 1, :, cols])
        for o in range(1, T):
            dest = lax.rem(t + o, T)
            tps[n, o] = pltpu.make_async_remote_copy(
                acc.at[n, pl.ds(pl.multiple_of(dest * mt, mt), mt)], tin.at[n, o - 1],
                tp_s.at[n, o], tp_r.at[n, o], device_id={"tp": dest}, device_id_type=MESH,
            )
            tps[n, o].start()
    for n in range(nb):
        result = acc[n, pl.ds(pl.multiple_of(t * mt, mt), mt), :]
        for o in range(1, T):
            tps[n, o].wait()
            result = result + tin[n, o - 1]
        out_ref[:, n * nc : (n + 1) * nc] = result.astype(BF16)
    for cp in sends:
        cp.wait_send()


def body(
    sizes,
    hidden,
    w_query,
    w_key,
    w_value,
    b_query,
    b_key,
    b_value,
    w_out,
    prefix_keys,
    prefix_values,
    suffix_keys,
    suffix_values,
    suffix_lengths,
    prompt_of,
):
    R, S, T = sizes
    M, K = hidden.shape
    q_heads, kvh = w_query.shape[1] // HD, w_key.shape[1] // HD
    prompts, pre, _ = prefix_keys.shape
    per, suf, _ = suffix_keys.shape
    N = w_out.shape[1]
    qhalf = q_heads // S
    kvw = max(kvh // S, 1)
    gq = qhalf // kvw
    rz = per * GUESS
    nb = 2 if N % (2 * HD) == 0 else 1
    dims = dict(
        R=R, T=T, M=M, kvw=kvw, gq=gq, rz=rz, kvh=kvh, qhalf=qhalf, pre=pre, suf=suf,
        prompts=prompts, per=per, prefix_total=pre * R * S, nb=nb,
    )
    W, gw, L = kvw * HD, gq * HD, gq * rz
    cw = gw + 2 * HD
    steps = np.arange(HD // 2).astype(np.float32) * np.float32(2.0 / HD)
    freqs = np.exp(np.float32(-math.log(ROPE_BASE)) * steps).astype(np.float32)
    freqs = jnp.asarray(np.concatenate([freqs, freqs])[None])
    smem = pl.BlockSpec(memory_space=pltpu.SMEM)
    vmem = pl.BlockSpec(memory_space=pltpu.VMEM)
    hbm = pl.BlockSpec(memory_space=pl.ANY)
    dma = pltpu.SemaphoreType.DMA
    return pl.pallas_call(
        functools.partial(kernel, dims),
        out_shape=jax.ShapeDtypeStruct((M // T, N), BF16),
        in_specs=[smem, smem] + [vmem] * 4 + [hbm] * 9,
        out_specs=vmem,
        scratch_shapes=[
            pltpu.VMEM((M, K), BF16),
            pltpu.VMEM((S, kvw, K, gw), BF16),
            pltpu.VMEM((S, K, W), BF16),
            pltpu.VMEM((S, K, W), BF16),
            pltpu.VMEM((S, kvw, gw, N), BF16),
            pltpu.VMEM((S, prompts, pre, W), BF16),
            pltpu.VMEM((S, prompts, pre, W), BF16),
            pltpu.VMEM((S, per, suf, W), BF16),
            pltpu.VMEM((S, per, suf, W), BF16),
            pltpu.VMEM((kvw, prompts * HD, S * pre), BF16),
            pltpu.VMEM((kvw, per * HD, S * suf), BF16),
            pltpu.VMEM((kvw, M, cw), F32),
            pltpu.VMEM((kvw, M, cw), F32),
            pltpu.VMEM((kvw, M, cw), F32),
            pltpu.VMEM((kvw, M, cw + HD), jnp.int16),
            pltpu.VMEM((kvw, R, rz, cw + HD), jnp.int16),
            pltpu.VMEM((kvw, R, gq, rz, HD), BF16),
            pltpu.VMEM((kvw, rz, HD), F32),
            pltpu.VMEM((kvw, rz, HD), F32),
            pltpu.VMEM((kvw, HD, L), F32),
            pltpu.VMEM((kvw, 8, L), F32),
            pltpu.VMEM((kvw, R, HD, L), BF16),
            pltpu.VMEM((kvw, R, HD, L), BF16),
            pltpu.VMEM((kvw, R, 8, L), F32),
            pltpu.VMEM((kvw, R, 8, L), F32),
            pltpu.VMEM((S, kvw, M, gw), BF16),
            pltpu.VMEM((nb, M, N // nb), F32),
            pltpu.VMEM((nb, max(T - 1, 1), M // T, N // nb), F32),
            pltpu.VMEM((1, q_heads * HD), F32),
            pltpu.VMEM((1, kvh * HD), F32),
            pltpu.VMEM((1, kvh * HD), F32),
            dma((9,)),
            dma((S, kvw)),
            dma((S, kvw)),
            dma((4,)),
            dma((4,)),
            dma((kvw,)),
            dma((kvw,)),
        ]
        + [dma((kvw, R))] * 12
        + [dma((nb, T))] * 2,
        compiler_params=pltpu.CompilerParams(
            collective_id=0, has_side_effects=True, vmem_limit_bytes=60 * 1024 * 1024
        ),
        cost_estimate=pl.CostEstimate(
            flops=2 * M * K * (w_query.shape[1] + 2 * w_key.shape[1]) + 2 * M * N * w_out.shape[0],
            bytes_accessed=2 * (w_query.size + 2 * w_key.size + w_out.size)
            + 4 * (prefix_keys.size + suffix_keys.size),
            transcendentals=0,
        ),
    )(
        suffix_lengths,
        prompt_of,
        freqs,
        b_query,
        b_key,
        b_value,
        hidden,
        w_query,
        w_key,
        w_value,
        w_out,
        prefix_keys,
        prefix_values,
        suffix_keys,
        suffix_values,
    )


def solution(mesh):
    sizes = (mesh.shape["roll"], mesh.shape["seq"], mesh.shape["tp"])
    return jax.shard_map(
        functools.partial(body, sizes),
        mesh=mesh,
        in_specs=(
            P("groups", ("roll", "seq")),
            P(("roll", "seq"), "tp"),
            P(("roll", "seq"), "tp"),
            P(("roll", "seq"), "tp"),
            P("tp"),
            P("tp"),
            P("tp"),
            P("tp", ("roll", "seq")),
            P("groups", ("roll", "seq"), "tp"),
            P("groups", ("roll", "seq"), "tp"),
            P(("groups", "roll"), "seq", "tp"),
            P(("groups", "roll"), "seq", "tp"),
            P("groups"),
            P("groups"),
        ),
        out_specs=P(("groups", "tp"), ("roll", "seq")),
        check_vma=False,
    )
```

```python
import functools
import math

import jax
import jax.numpy as jnp
import numpy as np
from jax import lax
from jax.experimental import pallas as pl
from jax.experimental.pallas import tpu as pltpu
from jax.sharding import PartitionSpec as P

HD = 128
GUESS = 8
ROPE_BASE = 1000000.0
NEG_FILL = -1e30
SCALE = math.log2(math.e) / math.sqrt(HD)
MESH = pl.DeviceIdType.MESH
F32 = jnp.float32
BF16 = jnp.bfloat16


def dot(a, b):
    return jnp.dot(a, b, preferred_element_type=F32)


def dot_nt(a, b):
    return lax.dot_general(a, b, (((1,), (1,)), ((), ())), preferred_element_type=F32)


def kernel(
    dims,
    lens_ref,
    prompt_ref,
    freq_ref,
    bq_ref,
    bk_ref,
    bv_ref,
    hid_ref,
    wq_ref,
    wk_ref,
    wv_ref,
    wo_ref,
    pk_ref,
    pv_ref,
    sk_ref,
    sv_ref,
    out_ref,
    hid,
    wq,
    wk,
    wv,
    wo,
    kb,
    vb,
    skb,
    svb,
    vt,
    svt,
    sibout,
    sibin,
    zs,
    zq,
    zin,
    qg,
    kn,
    vn,
    onum,
    ostat,
    nsend,
    nin,
    stsend,
    stin,
    att,
    acc,
    accb,
    tin,
    bq,
    bk,
    bv,
    ld,
    ldw,
    ldo,
    sw_s,
    sw_r,
    pr_s,
    pr_r,
    rs_s,
    rs_r,
    ag_s,
    ag_r,
    nu_s,
    nu_r,
    st_s,
    st_r,
    at_s,
    at_r,
    fw_s,
    fw_r,
    tp_s,
    tp_r,
):
    R, T = dims["R"], dims["T"]
    kvw, gq, rz, M = dims["kvw"], dims["gq"], dims["rz"], dims["M"]
    kvh, qhalf, pre, suf = dims["kvh"], dims["qhalf"], dims["pre"], dims["suf"]
    prompts, per = dims["prompts"], dims["per"]
    gw = gq * HD
    cw = gw + 2 * HD
    W = kvw * HD
    L = gq * rz
    mt = M // T
    z = lax.axis_index("roll")
    c = lax.axis_index("seq")
    t = lax.axis_index("tp")
    sib = 1 - c

    def kv_off(core):
        if kvh >= 2:
            return pl.multiple_of(core * W, HD)
        return 0

    def q_off(core, k):
        return pl.multiple_of((core * qhalf + k * gq) * HD, HD)

    halves = (sib, c)
    hk = gq + 2
    biases = ((bq_ref, bq), (bk_ref, bk), (bv_ref, bv))

    loads = [pltpu.make_async_copy(hid_ref, hid, ld.at[0])]
    loads[0].start()
    wload = {}
    for k in range(kvw):
        for s in range(2):
            cols = pl.ds(q_off(halves[s], k), gw)
            wload[s, k] = pltpu.make_async_copy(wq_ref.at[:, cols], wq.at[s, k], ldw.at[s, k])
            wload[s, k].start()
            if k == 0:
                cols = pl.ds(kv_off(halves[s]), W)
                for src, dst, i in ((wk_ref, wk, 1), (wv_ref, wv, 3)):
                    cp = pltpu.make_async_copy(src.at[:, cols], dst.at[s], ld.at[i + s])
                    cp.start()
                    loads.append(cp)

    barrier = pltpu.get_barrier_semaphore()
    for o in range(1, R):
        pl.semaphore_signal(
            barrier, inc=1, device_id={"roll": lax.rem(z + o, R)}, device_id_type=MESH
        )
    pl.semaphore_signal(barrier, inc=1, device_id={"seq": sib}, device_id_type=MESH)
    for o in range(1, T):
        pl.semaphore_signal(
            barrier, inc=1, device_id={"tp": lax.rem(t + o, T)}, device_id_type=MESH
        )
    pl.semaphore_wait(barrier, R + T - 1)

    def project(s, k):
        x = hid[...]
        cols = slice(k * HD, (k + 1) * HD)
        return dot(x, wq[s, k]), dot(x, wk[s, :, cols]), dot(x, wv[s, :, cols])

    def other_half(k):
        wload[0, k].wait()
        if k == 0:
            loads[1].wait()
            loads[2].wait()
        a, b, d = project(0, k)
        sibout[k, :, 0:gw] = a
        sibout[k, :, gw : gw + HD] = b
        sibout[k, :, gw + HD : cw] = d
        cp = pltpu.make_async_remote_copy(
            sibout.at[k], sibin.at[k], pr_s.at[k], pr_r.at[k],
            device_id={"seq": sib}, device_id_type=MESH,
        )
        cp.start()
        return cp

    def own_half(k):
        wload[1, k].wait()
        if k == 0:
            loads[3].wait()
            loads[4].wait()
        a, b, d = project(1, k)
        zs[k, :, 0:gw] = a
        zs[k, :, gw : gw + HD] = b
        zs[k, :, gw + HD : cw] = d

    loads[0].wait()
    pairs = [other_half(0)]
    own_half(0)
    for k in range(1, kvw):
        pairs.append(other_half(k))

    kv_local, kv_remote = [], []
    for i, (src, dst) in enumerate(((pk_ref, kb), (pv_ref, vb), (sk_ref, skb), (sv_ref, svb))):
        cp = pltpu.make_async_copy(
            src.at[:, :, pl.ds(kv_off(c), W)], dst.at[0], ld.at[5 + i]
        )
        cp.start()
        kv_local.append(cp)
        cp = pltpu.make_async_remote_copy(
            src.at[:, :, pl.ds(kv_off(sib), W)], dst.at[1], sw_s.at[i], sw_r.at[i],
            device_id={"seq": sib}, device_id_type=MESH,
        )
        if i < 2:
            cp.start()
        kv_remote.append(cp)
    oload = {}
    for s, half in ((0, c), (1, sib)):
        for k in range(kvw):
            oload[s, k] = pltpu.make_async_copy(
                wo_ref.at[pl.ds(q_off(half, k), gw)], wo.at[s, k], ldo.at[s, k]
            )
            oload[s, k].start()

    def along(src_of, dst_of, sems, semr, o):
        dest = lax.rem(z + o, R)
        return pltpu.make_async_remote_copy(
            src_of(dest), dst_of(z), sems, semr, device_id={"roll": dest}, device_id_type=MESH
        )

    def arrived(dst_of, sems, semr, o):
        source = lax.rem(z + R - o, R)
        ref = dst_of(source)
        pltpu.make_async_remote_copy(
            ref, ref, sems, semr, device_id={"roll": lax.rem(z + o, R)}, device_id_type=MESH
        ).wait_recv()
        return source

    sends = []

    wlane = lax.broadcasted_iota(jnp.int32, (M, HD), 1)
    for k in range(kvw):
        if k > 0:
            own_half(k)
        pairs[k].wait()
        powers = jnp.zeros((M, HD), F32)
        for h in range(hk):
            cols = slice(h * HD, (h + 1) * HD)
            x = zs[k, :, cols] + sibin[k, :, cols]
            zs[k, :, cols] = x
            largest = jnp.maximum(jnp.max(jnp.abs(x), axis=1, keepdims=True), 1e-30)
            power = jnp.ceil(jnp.log2(largest) + 0.01)
            code = jnp.round(x * (32767.0 / jnp.exp2(power)))
            zq[k, :, cols] = code.astype(jnp.int32).astype(jnp.int16)
            powers = jnp.where(wlane == h, power, powers)
        zq[k, :, cw : cw + HD] = powers.astype(jnp.int32).astype(jnp.int16)
        for o in range(1, R):
            cp = along(
                lambda dest, k=k: zq.at[k, pl.ds(pl.multiple_of(dest * rz, rz), rz)],
                lambda me, k=k: zin.at[k, me],
                rs_s.at[k, o], rs_r.at[k, o], o,
            )
            cp.start()
            sends.append(cp)
    for cp in kv_remote[2:]:
        cp.start()
    for src, dst in biases:
        dst[...] = src[...].astype(F32).reshape(dst.shape)

    tok = lax.broadcasted_iota(jnp.int32, (rz, HD), 0)
    base = jnp.zeros((rz, HD), jnp.int32)
    for i in range(per):
        base = jnp.where(tok // GUESS == i, lens_ref[z * per + i], base)
    position = (dims["prefix_total"] + base + tok % GUESS).astype(F32)
    angles = position * freq_ref[...]
    cosine = jnp.cos(angles)
    lane = lax.broadcasted_iota(jnp.int32, (rz, HD), 1)
    sine = jnp.sin(angles)
    sine = jnp.where(lane < HD // 2, -sine, sine)

    def rotate(x):
        return x * cosine + pltpu.roll(x, HD // 2, 1) * sine

    def turn(src, dst, s):
        count, length = src.shape[1], src.shape[2]
        for k in range(kvw):
            cols = slice(k * HD, (k + 1) * HD)
            for p in range(count):
                dst[k, p * HD : (p + 1) * HD, s * length : (s + 1) * length] = src[s, p, :, cols].T

    for cp in kv_local:
        cp.wait()
    turn(vb, vt, 0)
    turn(svb, svt, 0)

    def finish(k):
        for o in range(1, R):
            arrived(lambda src, k=k: zin.at[k, src], rs_s.at[k, o], rs_r.at[k, o], o)
        x = zs[k, pl.ds(pl.multiple_of(z * rz, rz), rz), :]
        sums = [x[:, h * HD : (h + 1) * HD] for h in range(hk)]
        for o in range(1, R):
            got = zin[k, lax.rem(z + R - o, R)].astype(jnp.int32).astype(F32)
            units = jnp.exp2(got[:, cw:]) * (1.0 / 32767.0)
            for h in range(hk):
                sums[h] = sums[h] + got[:, h * HD : (h + 1) * HD] * units[:, h : h + 1]
        x = jnp.concatenate(sums, axis=1)
        xq = x[:, :gw] + bq[:, pl.ds(q_off(c, k), gw)]
        kcol = pl.ds(pl.multiple_of(kv_off(c) + k * HD, HD), HD)
        for h in range(gq):
            qg[k, z, h] = rotate(xq[:, h * HD : (h + 1) * HD]).astype(BF16)
        for o in range(1, R):
            cp = along(
                lambda dest, k=k: qg.at[k, z], lambda me, k=k: qg.at[k, me],
                ag_s.at[k, o], ag_r.at[k, o], o,
            )
            cp.start()
            sends.append(cp)
        kn[k] = rotate(x[:, gw : gw + HD] + bk[:, kcol])
        vn[k] = x[:, gw + HD :] + bv[:, kcol]

    toks = lax.broadcasted_iota(jnp.int32, (rz, HD), 0)
    parts = [(toks // GUESS == i).astype(F32).astype(BF16) for i in range(per)]
    ltok = lax.broadcasted_iota(jnp.int32, (1, L), 1) % rz
    live = jnp.zeros((1, L), jnp.int32)
    for i in range(per):
        live = jnp.where(ltok // GUESS == i, lens_ref[z * per + i], live)

    def own_rows(k):
        cols = slice(k * HD, (k + 1) * HD)
        q = qg[k, z]
        keys = jnp.concatenate(
            [jnp.concatenate([skb[s, p, :, cols] for p in range(per)], axis=1) for s in range(2)],
            axis=0,
        )
        qs = jnp.concatenate([(q * m[None]).reshape(L, HD) for m in parts], axis=1)
        s_suf = dot_nt(keys, qs)
        place = lax.broadcasted_iota(jnp.int32, (suf, L), 0)
        s_suf = jnp.concatenate(
            [
                jnp.where(place < live - half * suf, s_suf[s * suf : (s + 1) * suf], NEG_FILL)
                for s, half in ((0, c), (1, sib))
            ],
            axis=0,
        )
        s_new = dot_nt(kn[k].astype(BF16), q.reshape(L, HD))
        row = lax.broadcasted_iota(jnp.int32, (rz, L), 0)
        col = lax.broadcasted_iota(jnp.int32, (rz, L), 1) % rz
        seen = (row // GUESS == col // GUESS) & (row % GUESS <= col % GUESS)
        s_new = jnp.where(seen, s_new, NEG_FILL)
        peak = jnp.maximum(
            jnp.max(s_suf, axis=0, keepdims=True), jnp.max(s_new, axis=0, keepdims=True)
        )
        w_suf = jnp.exp2((s_suf - peak) * SCALE)
        w_new = jnp.exp2((s_new - peak) * SCALE)
        both = dot(svt[k], w_suf.astype(BF16))
        numer = dot(vn[k].T.astype(BF16), w_new.astype(BF16))
        for i in range(per):
            numer = numer + jnp.where(ltok // GUESS == i, both[i * HD : (i + 1) * HD], 0.0)
        onum[k] = numer
        ostat[k, 0:1, :] = peak
        ostat[k, 1:2, :] = jnp.sum(w_suf, axis=0, keepdims=True) + jnp.sum(
            w_new, axis=0, keepdims=True
        )

    zb = max(1, min(R, 256 // L))

    def every_row(k):
        cols = slice(k * HD, (k + 1) * HD)
        keys = jnp.concatenate(
            [
                jnp.concatenate([kb[s, p, :, cols] for p in range(prompts)], axis=1)
                for s in range(2)
            ],
            axis=0,
        )
        for first in range(0, R, zb):
            blocks = []
            places = []
            for o in range(first, first + zb):
                if o == 0:
                    places.append(z)
                else:
                    places.append(
                        arrived(lambda src, k=k: qg.at[k, src], ag_s.at[k, o], ag_r.at[k, o], o)
                    )
            pick = jnp.zeros((1, zb * L), jnp.int32)
            wide = lax.broadcasted_iota(jnp.int32, (1, zb * L), 1)
            for j in range(zb):
                owner = jnp.zeros((rz, HD), jnp.int32)
                for i in range(per):
                    which = prompt_ref[places[j] * per + i]
                    owner = jnp.where(toks // GUESS == i, which, owner)
                    here = (wide // L == j) & ((wide % rz) // GUESS == i)
                    pick = jnp.where(here, which, pick)
                q = qg[k, places[j]]
                blocks.append(
                    jnp.concatenate(
                        [
                            (q * (owner == p).astype(F32).astype(BF16)[None]).reshape(L, HD)
                            for p in range(prompts)
                        ],
                        axis=1,
                    )
                )
            s_pre = dot_nt(keys, jnp.concatenate(blocks, axis=0))
            peak = jnp.max(s_pre, axis=0, keepdims=True)
            w_pre = jnp.exp2((s_pre - peak) * SCALE)
            total = jnp.sum(w_pre, axis=0, keepdims=True)
            both = dot(vt[k], w_pre.astype(BF16))
            numer = jnp.zeros((HD, zb * L), F32)
            for p in range(prompts):
                numer = jnp.where(pick == p, both[p * HD : (p + 1) * HD], numer)
            numer = numer.astype(BF16)
            for j in range(zb):
                nsend[k, places[j]] = numer[:, j * L : (j + 1) * L]
                stsend[k, places[j], 0:1, :] = peak[:, j * L : (j + 1) * L]
                stsend[k, places[j], 1:2, :] = total[:, j * L : (j + 1) * L]
                o = R - first - j
                if o == R:
                    continue
                cp = along(
                    lambda dest, k=k: nsend.at[k, dest], lambda me, k=k: nin.at[k, me],
                    nu_s.at[k, o], nu_r.at[k, o], o,
                )
                cp.start()
                sends.append(cp)
                cp = along(
                    lambda dest, k=k: stsend.at[k, dest], lambda me, k=k: stin.at[k, me],
                    st_s.at[k, o], st_r.at[k, o], o,
                )
                cp.start()
                sends.append(cp)

    finish(0)
    for cp in kv_remote[:2]:
        cp.wait()
    turn(vb, vt, 1)
    for k in range(1, kvw):
        finish(k)
    for k in range(kvw):
        every_row(k)
    for cp in kv_remote[2:]:
        cp.wait()
    turn(svb, svt, 1)

    forwards = {}

    def forward(k, o, place):
        rows = pl.ds(pl.multiple_of(place * rz, rz), rz)
        cp = pltpu.make_async_remote_copy(
            att.at[0, k, rows], att.at[1, k, rows], fw_s.at[k, o], fw_r.at[k, o],
            device_id={"seq": sib}, device_id_type=MESH,
        )
        cp.start()
        forwards[k, o] = cp

    def combine(k):
        for o in range(1, R):
            arrived(lambda src, k=k: nin.at[k, src], nu_s.at[k, o], nu_r.at[k, o], o)
            arrived(lambda src, k=k: stin.at[k, src], st_s.at[k, o], st_r.at[k, o], o)
        stats = [(ostat[k, 0:1, :], ostat[k, 1:2, :]), (stsend[k, z, 0:1, :], stsend[k, z, 1:2, :])]
        numers = [onum[k], nsend[k, z].astype(F32)]
        for o in range(1, R):
            source = lax.rem(z + R - o, R)
            stats.append((stin[k, source, 0:1, :], stin[k, source, 1:2, :]))
            numers.append(nin[k, source].astype(F32))
        top = functools.reduce(jnp.maximum, [peak for peak, _ in stats])
        total = jnp.zeros((1, L), F32)
        numer = jnp.zeros((HD, L), F32)
        for (peak, part), piece in zip(stats, numers):
            factor = jnp.exp2((peak - top) * SCALE)
            total = total + part * factor
            numer = numer + piece * factor
        share = (numer / total).T.astype(BF16)
        mine = pl.ds(pl.multiple_of(z * rz, rz), rz)
        att[0, k, mine, :] = jnp.concatenate(
            [share[h * rz : (h + 1) * rz] for h in range(gq)], axis=1
        )
        for o in range(1, R):
            cp = along(
                lambda dest, k=k: att.at[0, k, mine],
                lambda me, k=k: att.at[0, k, pl.ds(pl.multiple_of(me * rz, rz), rz)],
                at_s.at[k, o], at_r.at[k, o], o,
            )
            cp.start()
            sends.append(cp)
        forward(k, 0, z)

    for k in range(kvw):
        own_rows(k)
        combine(k)

    total = jnp.zeros((M, dims["nb"] * acc.shape[2]), F32)
    for k in range(kvw):
        for o in range(1, R):
            source = arrived(
                lambda src, k=k: att.at[0, k, pl.ds(pl.multiple_of(src * rz, rz), rz)],
                at_s.at[k, o], at_r.at[k, o], o,
            )
            forward(k, o, source)
        oload[0, k].wait()
        total = total + dot(att[0, k], wo[0, k])
        for o in range(R):
            forwards[k, o].wait()
        oload[1, k].wait()
        if k < kvw - 1:
            total = total + dot(att[1, k], wo[1, k])
    nb, nc = dims["nb"], acc.shape[2]
    tps = {}
    for n in range(nb):
        cols = slice(n * nc, (n + 1) * nc)
        piece = total[:, cols] + dot(att[1, kvw - 1], wo[1, kvw - 1, :, cols])
        acc[n] = piece
        accb[n] = piece.astype(BF16)
        for o in range(1, T):
            dest = lax.rem(t + o, T)
            tps[n, o] = pltpu.make_async_remote_copy(
                accb.at[n, pl.ds(pl.multiple_of(dest * mt, mt), mt)], tin.at[n, o - 1],
                tp_s.at[n, o], tp_r.at[n, o], device_id={"tp": dest}, device_id_type=MESH,
            )
            tps[n, o].start()
    for n in range(nb):
        result = acc[n, pl.ds(pl.multiple_of(t * mt, mt), mt), :]
        for o in range(1, T):
            tps[n, o].wait()
            result = result + tin[n, o - 1].astype(F32)
        out_ref[:, n * nc : (n + 1) * nc] = result.astype(BF16)
    for cp in sends:
        cp.wait_send()


def body(
    sizes,
    hidden,
    w_query,
    w_key,
    w_value,
    b_query,
    b_key,
    b_value,
    w_out,
    prefix_keys,
    prefix_values,
    suffix_keys,
    suffix_values,
    suffix_lengths,
    prompt_of,
):
    R, S, T = sizes
    M, K = hidden.shape
    q_heads, kvh = w_query.shape[1] // HD, w_key.shape[1] // HD
    prompts, pre, _ = prefix_keys.shape
    per, suf, _ = suffix_keys.shape
    N = w_out.shape[1]
    qhalf = q_heads // S
    kvw = max(kvh // S, 1)
    gq = qhalf // kvw
    rz = per * GUESS
    nb = 2 if N % (2 * HD) == 0 else 1
    dims = dict(
        R=R, T=T, M=M, kvw=kvw, gq=gq, rz=rz, kvh=kvh, qhalf=qhalf, pre=pre, suf=suf,
        prompts=prompts, per=per, prefix_total=pre * R * S, nb=nb,
    )
    W, gw, L = kvw * HD, gq * HD, gq * rz
    cw = gw + 2 * HD
    steps = np.arange(HD // 2).astype(np.float32) * np.float32(2.0 / HD)
    freqs = np.exp(np.float32(-math.log(ROPE_BASE)) * steps).astype(np.float32)
    freqs = jnp.asarray(np.concatenate([freqs, freqs])[None])
    smem = pl.BlockSpec(memory_space=pltpu.SMEM)
    vmem = pl.BlockSpec(memory_space=pltpu.VMEM)
    hbm = pl.BlockSpec(memory_space=pl.ANY)
    dma = pltpu.SemaphoreType.DMA
    return pl.pallas_call(
        functools.partial(kernel, dims),
        out_shape=jax.ShapeDtypeStruct((M // T, N), BF16),
        in_specs=[smem, smem] + [vmem] * 4 + [hbm] * 9,
        out_specs=vmem,
        scratch_shapes=[
            pltpu.VMEM((M, K), BF16),
            pltpu.VMEM((S, kvw, K, gw), BF16),
            pltpu.VMEM((S, K, W), BF16),
            pltpu.VMEM((S, K, W), BF16),
            pltpu.VMEM((S, kvw, gw, N), BF16),
            pltpu.VMEM((S, prompts, pre, W), BF16),
            pltpu.VMEM((S, prompts, pre, W), BF16),
            pltpu.VMEM((S, per, suf, W), BF16),
            pltpu.VMEM((S, per, suf, W), BF16),
            pltpu.VMEM((kvw, prompts * HD, S * pre), BF16),
            pltpu.VMEM((kvw, per * HD, S * suf), BF16),
            pltpu.VMEM((kvw, M, cw), F32),
            pltpu.VMEM((kvw, M, cw), F32),
            pltpu.VMEM((kvw, M, cw), F32),
            pltpu.VMEM((kvw, M, cw + HD), jnp.int16),
            pltpu.VMEM((kvw, R, rz, cw + HD), jnp.int16),
            pltpu.VMEM((kvw, R, gq, rz, HD), BF16),
            pltpu.VMEM((kvw, rz, HD), F32),
            pltpu.VMEM((kvw, rz, HD), F32),
            pltpu.VMEM((kvw, HD, L), F32),
            pltpu.VMEM((kvw, 8, L), F32),
            pltpu.VMEM((kvw, R, HD, L), BF16),
            pltpu.VMEM((kvw, R, HD, L), BF16),
            pltpu.VMEM((kvw, R, 8, L), F32),
            pltpu.VMEM((kvw, R, 8, L), F32),
            pltpu.VMEM((S, kvw, M, gw), BF16),
            pltpu.VMEM((nb, M, N // nb), F32),
            pltpu.VMEM((nb, M, N // nb), BF16),
            pltpu.VMEM((nb, max(T - 1, 1), M // T, N // nb), BF16),
            pltpu.VMEM((1, q_heads * HD), F32),
            pltpu.VMEM((1, kvh * HD), F32),
            pltpu.VMEM((1, kvh * HD), F32),
            dma((9,)),
            dma((S, kvw)),
            dma((S, kvw)),
            dma((4,)),
            dma((4,)),
            dma((kvw,)),
            dma((kvw,)),
        ]
        + [dma((kvw, R))] * 12
        + [dma((nb, T))] * 2,
        compiler_params=pltpu.CompilerParams(
            collective_id=0, has_side_effects=True, vmem_limit_bytes=60 * 1024 * 1024
        ),
        cost_estimate=pl.CostEstimate(
            flops=2 * M * K * (w_query.shape[1] + 2 * w_key.shape[1]) + 2 * M * N * w_out.shape[0],
            bytes_accessed=2 * (w_query.size + 2 * w_key.size + w_out.size)
            + 4 * (prefix_keys.size + suffix_keys.size),
            transcendentals=0,
        ),
    )(
        suffix_lengths,
        prompt_of,
        freqs,
        b_query,
        b_key,
        b_value,
        hidden,
        w_query,
        w_key,
        w_value,
        w_out,
        prefix_keys,
        prefix_values,
        suffix_keys,
        suffix_values,
    )


def solution(mesh):
    sizes = (mesh.shape["roll"], mesh.shape["seq"], mesh.shape["tp"])
    return jax.shard_map(
        functools.partial(body, sizes),
        mesh=mesh,
        in_specs=(
            P("groups", ("roll", "seq")),
            P(("roll", "seq"), "tp"),
            P(("roll", "seq"), "tp"),
            P(("roll", "seq"), "tp"),
            P("tp"),
            P("tp"),
            P("tp"),
            P("tp", ("roll", "seq")),
            P("groups", ("roll", "seq"), "tp"),
            P("groups", ("roll", "seq"), "tp"),
            P(("groups", "roll"), "seq", "tp"),
            P(("groups", "roll"), "seq", "tp"),
            P("groups"),
            P("groups"),
        ),
        out_specs=P(("groups", "tp"), ("roll", "seq")),
        check_vma=False,
    )
```
